512 devices in a mesh: ctx: 64 (over y, z), head: 8 (over x, core).
Axes of the slice: x: 4, y: 4, z: 16, core: 2. Of those that a mesh axis runs over, the one named last changes fastest.
Arguments:
- queries: bfloat16 [65536, 3072], P('ctx', 'head'), may hold values from -20 to 20
- keys: bfloat16 [65536, 3072], P('ctx', 'head'), may hold values from -20 to 20
- values: bfloat16 [65536, 3072], P('ctx', 'head'), may hold values from -6 to 6
- block_mask: int32 [128, 128], replicated, may hold values from 0 to 1, as said below
- head_labels: int32 [24], replicated, may hold values from 0 to 1, as said below
- w_out: bfloat16 [3072, 3072], P('ctx', 'head'), may hold values from -0.109375 to 0.109375
Outputs:
- projected: bfloat16 [65536, 3072], P('ctx', 'head')
The draws below stay inside these ranges and needn't reach their ends.
Inputs may be any that keep to these rules, and one draw needn't show every extreme that they name: block_mask is 1 only where |a - b| <= 2 or where b = 0 and a > 2; every diagonal entry is 1. `head_labels`: among the 3 heads of each group of consecutive heads, between 1 and 2 are temporal, and some group has exactly 2.
All inputs are finite; a program needn't handle non-finite values.
Results may differ from the reference program's by a relative error of at most 0.0057.
Values may be sent and summed in bfloat16 or wider, within the bound.
No kernel may reach another device: no remote copies, remote signals or barrier semaphores. Data moves between devices by JAX's collectives and lax.ppermute only.
A program may use at most 128 MiB of HBM per device.

```python
import math
import jax
import jax.numpy as jnp
from jax import lax

HEADS = 24
HEAD_DIM = 128
D = 3072
BLOCK = 512
REACH = 2
HEAD_DEV = 3
TEMP_DEV = 2
FRAMES = 32
POS = 2048
TOKENS = 65536
NB = 128


def draw_queries(key, part):
    key = jax.random.fold_in(key, 3)
    drawn = jnp.clip(jax.random.normal(key, (TOKENS, D), jnp.float32), -4.0, 4.0)
    result = drawn
    return result.astype(jnp.bfloat16)


def draw_keys(key, part):
    key = jax.random.fold_in(key, 5)
    drawn = jnp.clip(jax.random.normal(key, (TOKENS, D), jnp.float32), -4.0, 4.0)
    result = drawn
    return result.astype(jnp.bfloat16)


def draw_block_mask(key, part):
    key = jax.random.fold_in(key, 11)
    rows = jnp.arange(NB, dtype=jnp.int32)[:, None]
    cols = jnp.arange(NB, dtype=jnp.int32)[None, :]
    coin = jax.random.randint(key, (NB, NB), 0, 4) < 3
    band = jnp.abs(rows - cols) <= REACH
    keep = band & (coin | (rows == cols))
    first = (cols == 0) & (rows > REACH) & coin
    return (keep | first).astype(jnp.int32)


def draw_head_labels(key, part):
    key = jax.random.fold_in(key, 7)
    groups = HEADS // HEAD_DEV
    k1, k2, k3 = jax.random.split(key, 3)
    counts = jax.random.randint(k1, (groups,), 1, TEMP_DEV + 1)
    full_group = jax.random.randint(k2, (), 0, groups)
    counts = jnp.where(jnp.arange(groups) == full_group, TEMP_DEV, counts)
    scores = jax.random.randint(k3, (groups, HEAD_DEV), 0, 1 << 20) * HEAD_DEV + jnp.arange(HEAD_DEV, dtype=jnp.int32)[None, :]
    rank = jnp.argsort(jnp.argsort(scores, axis=1), axis=1)
    return (rank < counts[:, None]).astype(jnp.int32).reshape(HEADS)


def block_levels(stream_key, dims, shards, smallest, largest):
    factor_of = 1.0
    for dim, parts in shards:
        steps = jax.random.uniform(jax.random.fold_in(jax.random.fold_in(stream_key, 6), dim), (parts,), jnp.float32, smallest / len(shards), largest / len(shards))
        factor_of = factor_of * jnp.repeat(jnp.exp(steps), dims[dim] // parts).reshape((-1,) + (1,) * (len(dims) - 1 - dim))
    return factor_of


def noise(rng, dims, spread, reach, shards=(), kind=jnp.bfloat16):
    values = jax.random.normal(rng, dims, jnp.float32) * spread
    if len(shards) > 0:
        values = block_levels(rng, dims, shards, -0.22, 0.18) * values
    return jnp.clip(values, min=-reach, max=reach).astype(kind)


def setup_inputs(seed: int = 0) -> dict:
    splits = jax.random.split(jax.random.key(seed), 7)
    return {
        "queries": draw_queries(jax.random.fold_in(splits[6], 71), 0),
        "keys": draw_keys(jax.random.fold_in(splits[6], 71), 0),
        "values": noise(splits[2], (TOKENS, D), 1.0, 6.0, ((0, 64), (1, 8))),
        "block_mask": draw_block_mask(jax.random.fold_in(splits[6], 71), 0),
        "head_labels": draw_head_labels(jax.random.fold_in(splits[6], 71), 0),
        "w_out": noise(splits[5], (D, D), D ** -0.5, 0.109375, ((0, 64), (1, 8))),
    }


def to_positions(x):
    half = POS // 2
    return x.reshape(FRAMES, 2, half, -1).transpose(2, 0, 1, 3).reshape(TOKENS, -1)

def to_frames(x):
    half = POS // 2
    return x.reshape(half, FRAMES, 2, -1).transpose(1, 2, 0, 3).reshape(TOKENS, -1)

def attend_head(query, keyrow, valrow, block_mask):
    scale = 1.0 / math.sqrt(HEAD_DIM)
    qblocks = query.reshape(NB, BLOCK, HEAD_DIM)
    kblocks = keyrow.reshape(NB, BLOCK, HEAD_DIM)
    vblocks = valrow.reshape(NB, BLOCK, HEAD_DIM)
    offsets = jnp.arange(-REACH, REACH + 1, dtype=jnp.int32)

    def one_block(index):
        cand = index + offsets
        inside = (cand >= 0) & (cand < NB)
        safe = jnp.clip(cand, 0, NB - 1).astype(jnp.int32)
        row = block_mask[index]
        bits = inside & (row[safe] == 1)
        first = (index > REACH) & (row[0] == 1)
        picks = jnp.concatenate([safe, jnp.zeros((1,), jnp.int32)])
        allbits = jnp.concatenate([bits, first[None]])
        kcat = kblocks[picks].reshape(-1, HEAD_DIM)
        vcat = vblocks[picks].reshape(-1, HEAD_DIM)
        scores = jnp.dot(qblocks[index], kcat.T, preferred_element_type=jnp.float32) * scale
        columns = jnp.repeat(allbits, BLOCK)
        scores = jnp.where(columns[None, :], scores, -jnp.inf)
        top = lax.optimization_barrier(jnp.max(scores, axis=1, keepdims=True))
        weights = jnp.exp(scores - top)
        total = lax.optimization_barrier(jnp.sum(weights, axis=1, keepdims=True))
        mixed = jnp.dot(weights.astype(jnp.bfloat16), vcat, preferred_element_type=jnp.float32)
        return (mixed / total).astype(jnp.bfloat16)
    return lax.map(one_block, jnp.arange(NB, dtype=jnp.int32)).reshape(TOKENS, HEAD_DIM)

def reference(queries, keys, values, block_mask, head_labels, w_out):

    def per_head(head):
        start = head * HEAD_DIM
        query = lax.dynamic_slice_in_dim(queries, start, HEAD_DIM, 1)
        keyrow = lax.dynamic_slice_in_dim(keys, start, HEAD_DIM, 1)
        valrow = lax.dynamic_slice_in_dim(values, start, HEAD_DIM, 1)
        temporal = head_labels[head] == 1
        query = jnp.where(temporal, to_positions(query), query)
        keyrow = jnp.where(temporal, to_positions(keyrow), keyrow)
        valrow = jnp.where(temporal, to_positions(valrow), valrow)
        result = attend_head(query, keyrow, valrow, block_mask)
        return jnp.where(temporal, to_frames(result), result)
    heads_out = lax.map(per_head, jnp.arange(HEADS, dtype=jnp.int32))
    attn = heads_out.transpose(1, 0, 2).reshape(TOKENS, D)
    return jnp.dot(attn, w_out, preferred_element_type=jnp.float32).astype(jnp.bfloat16)
```

```python
import math

import jax
import jax.numpy as jnp
from jax import lax
from jax.experimental import pallas as pl
from jax.experimental.pallas import tpu as pltpu
from jax.sharding import PartitionSpec as P

HEAD_DIM = 128
BLOCK = 512
REACH = 2
BF = jnp.bfloat16
F32 = jnp.float32
RATE = math.log2(math.e) / math.sqrt(HEAD_DIM)
NEAR = ((0, 1, 2, 3, 4, 6), (1, 2, 3, 4, 5, 6))


def lanes(index):
    return slice(index * HEAD_DIM, (index + 1) * HEAD_DIM)


def attention_kernel(heads, bits, q_ref, own_ref, left_ref, right_ref, first_ref, out_ref, s_ref, m_ref, l_ref, acc_ref):
    sides = (left_ref, left_ref, own_ref, own_ref, right_ref, right_ref, first_ref)

    def tile(kind, place, slot):
        if place == 6:
            return first_ref[:, lanes(kind * heads + slot)]
        return sides[place][:, lanes((kind * 2 + place % 2) * heads + slot)]

    for slot in range(heads):
        for b in range(2):
            query = q_ref[:, lanes(b * heads + slot)]
            m_ref[...] = jnp.full_like(m_ref, -jnp.inf)
            l_ref[...] = jnp.zeros_like(l_ref)
            acc_ref[...] = jnp.zeros_like(acc_ref)
            for n, place in enumerate(NEAR[b]):

                @pl.when(bits[b, n] > 0)
                def _():
                    s = lax.dot_general(
                        query, tile(0, place, slot), (((1,), (1,)), ((), ())), preferred_element_type=F32
                    )
                    s_ref[n] = s
                    m = m_ref[...]
                    for c in range(BLOCK // HEAD_DIM):
                        m = jnp.maximum(m, s[:, lanes(c)])
                    m_ref[...] = m

            top = jnp.max(m_ref[...], axis=1, keepdims=True)
            m_ref[...] = jnp.broadcast_to(top, m_ref.shape)
            for n, place in enumerate(NEAR[b]):

                @pl.when(bits[b, n] > 0)
                def _():
                    peak = m_ref[...]
                    total = l_ref[...]
                    parts = []
                    for c in range(BLOCK // HEAD_DIM):
                        w = jnp.exp2((s_ref[n, :, lanes(c)] - peak) * RATE)
                        total = total + w
                        parts.append(w.astype(BF))
                    l_ref[...] = total
                    acc_ref[...] += jnp.dot(
                        jnp.concatenate(parts, axis=1), tile(1, place, slot), preferred_element_type=F32
                    )

            total = jnp.sum(l_ref[...], axis=1, keepdims=True)
            out_ref[:, lanes(b * heads + slot)] = (acc_ref[...] / total).astype(BF)


def attention(heads, bits, query, own, left, right, first):
    vmem = pl.BlockSpec(memory_space=pltpu.VMEM)
    pairs = heads * 2 * 6
    return pl.pallas_call(
        lambda *refs: attention_kernel(heads, *refs),
        out_shape=jax.ShapeDtypeStruct(query.shape, BF),
        in_specs=[pl.BlockSpec(memory_space=pltpu.SMEM)] + [vmem] * 5,
        out_specs=vmem,
        scratch_shapes=[
            pltpu.VMEM((6, BLOCK, BLOCK), F32),
            pltpu.VMEM((BLOCK, HEAD_DIM), F32),
            pltpu.VMEM((BLOCK, HEAD_DIM), F32),
            pltpu.VMEM((BLOCK, HEAD_DIM), F32),
        ],
        compiler_params=pltpu.CompilerParams(vmem_limit_bytes=40 << 20),
        cost_estimate=pl.CostEstimate(
            flops=pairs * 4 * BLOCK * BLOCK * HEAD_DIM,
            bytes_accessed=heads * 16 * BLOCK * HEAD_DIM * 2,
            transcendentals=pairs * BLOCK * BLOCK,
        ),
    )(bits, query, own, left, right, first)


def projection_kernel(groups, order, spatial_ref, mixed_ref, w_ref, out_ref):
    total = None
    for g in range(groups):
        rows = [
            w_ref[pl.ds(pl.multiple_of(order[g * 3 + slot] * HEAD_DIM, HEAD_DIM), HEAD_DIM), :] for slot in range(3)
        ]
        part = jnp.dot(
            mixed_ref[:, 2 * g * HEAD_DIM : 2 * (g + 1) * HEAD_DIM],
            jnp.concatenate(rows[:2], axis=0),
            preferred_element_type=F32,
        )
        part += jnp.dot(spatial_ref[:, lanes(g)], rows[2], preferred_element_type=F32)
        total = part if total is None else total + part
    out_ref[...] = total.astype(BF)


def projection(groups, order, spatial, mixed, w):
    vmem = pl.BlockSpec(memory_space=pltpu.VMEM)
    return pl.pallas_call(
        lambda *refs: projection_kernel(groups, *refs),
        out_shape=jax.ShapeDtypeStruct((spatial.shape[0], w.shape[1]), BF),
        in_specs=[pl.BlockSpec(memory_space=pltpu.SMEM)] + [vmem] * 3,
        out_specs=vmem,
        compiler_params=pltpu.CompilerParams(vmem_limit_bytes=40 << 20),
    )(order, spatial, mixed, w)


def slots_of(labels):
    temporal = labels == 1
    a = jnp.where(temporal[:, 0], 0, jnp.where(temporal[:, 1], 1, 2))
    c = jnp.where(~temporal[:, 2], 2, jnp.where(~temporal[:, 1], 1, 0))
    return jnp.stack([a, 3 - a - c, c], axis=1).astype(jnp.int32)


def split_blocks(x):
    return jnp.concatenate([x[:BLOCK], x[BLOCK:]], axis=1)


def position_pack(x, parts):
    rows = x.shape[0] // parts // 2
    return x.reshape(parts, 2, rows, x.shape[1]).transpose(0, 2, 1, 3).reshape(parts, rows, 2 * x.shape[1])


def exchange(x):
    return lax.all_to_all(x, "ctx", 0, 0, tiled=True)


def both_ways(x, count):
    left = lax.ppermute(x, "ctx", [(i, i + 1) for i in range(count - 1)])
    right = lax.ppermute(x, "ctx", [(i + 1, i) for i in range(count - 1)])
    return left, right


def scattered(x, place, count):
    step = count // 2
    while step >= 1:
        half = x.shape[0] // 2
        got = lax.ppermute(x[half:], "ctx", [(i, i + step) for i in range(0, count, 2 * step)])
        x = jnp.where(place % (2 * step) == step, got, x[:half])
        step //= 2
    return x


def gathered(x, count):
    for unit in (4, 1, 16):
        got = [lax.ppermute(x, "ctx", [(i, i ^ (unit * k)) for i in range(count)]) for k in (1, 2, 3)]
        x = jnp.concatenate([x] + got, axis=0)
    return x


def body(queries, keys, values, block_mask, head_labels, w_out):
    parts = lax.axis_size("ctx")
    groups = lax.axis_size("head")
    place = lax.axis_index("ctx")
    group = lax.axis_index("head")
    slots = slots_of(head_labels.reshape(groups, 3))
    mine = lax.dynamic_slice_in_dim(slots, group, 1, 0)[0]
    labels = lax.dynamic_slice_in_dim(head_labels, group * 3, 3)
    moves = lax.dynamic_slice_in_dim(labels, mine[1], 1)[0] == 1
    order = (slots + 3 * jnp.arange(groups, dtype=jnp.int32)[:, None]).reshape(-1)

    def head_of(x, slot):
        return lax.dynamic_slice_in_dim(x, mine[slot] * HEAD_DIM, HEAD_DIM, 1)

    weight_cols = lax.all_gather(w_out, "ctx", axis=0, tiled=True)

    q0, q1, q2 = (head_of(queries, s) for s in range(3))
    k0, k1, k2 = (head_of(keys, s) for s in range(3))
    v0, v1, v2 = (head_of(values, s) for s in range(3))

    index = place * 2 + jnp.arange(2, dtype=jnp.int32)
    total_blocks = block_mask.shape[0]
    rows = lax.dynamic_slice_in_dim(block_mask, place * 2, 2, 0)
    cand = index[:, None] + jnp.arange(-REACH, REACH + 1, dtype=jnp.int32)[None, :]
    every = jnp.arange(total_blocks, dtype=jnp.int32)
    hits = jnp.any((cand[:, :, None] == every[None, None, :]) & (rows[:, None, :] == 1), axis=2)
    first_bit = (index > REACH) & (rows[:, 0] == 1)
    bits = jnp.concatenate([hits, first_bit[:, None]], axis=1).astype(jnp.int32)

    pack_k = position_pack(jnp.concatenate([k0, k1], axis=1), parts)
    pack_v = position_pack(jnp.concatenate([v0, v1], axis=1), parts)
    moved_kv = exchange(jnp.concatenate([pack_k, pack_v], axis=2)).reshape(BLOCK, -1)
    moved_q = exchange(position_pack(jnp.concatenate([q0, q1], axis=1), parts)).reshape(BLOCK, -1)

    local = jnp.concatenate([k0, k1, v0, v1], axis=1)[: BLOCK // parts]
    shares = scattered(jnp.concatenate([k1, k2, v1, v2], axis=1)[:BLOCK], place, parts)
    piece = jnp.concatenate(
        [
            local[:, lanes(0)],
            jnp.where(moves, local[:, lanes(1)], shares[:, lanes(0)]),
            local[:, lanes(2)],
            jnp.where(moves, local[:, lanes(3)], shares[:, lanes(2)]),
            shares[:, lanes(1)],
            shares[:, lanes(3)],
        ],
        axis=1,
    )
    first = gathered(piece, parts)

    own2 = jnp.concatenate([split_blocks(k2), split_blocks(v2)], axis=1)
    left2, right2 = both_ways(own2, parts)
    out2 = attention(1, bits, split_blocks(q2), own2, left2, right2, first[:, 4 * HEAD_DIM :])
    attn2 = jnp.concatenate([out2[:, lanes(0)], out2[:, lanes(1)]], axis=0)
    spatial = lax.all_gather(attn2, "head", axis=1, tiled=True)

    def mix(moved, still, kinds):
        cols = []
        for n in range(kinds * 2):
            cols.append(moved[:, lanes(2 * n)])
            cols.append(jnp.where(moves, moved[:, lanes(2 * n + 1)], still[:, lanes(n)]))
        return jnp.concatenate(cols, axis=1)

    own = mix(moved_kv, jnp.concatenate([split_blocks(k1), split_blocks(v1)], axis=1), 2)
    left, right = both_ways(own, parts)
    query = mix(moved_q, split_blocks(q1), 1)
    out = attention(2, bits, query, own, left, right, first[:, : 4 * HEAD_DIM])

    back = exchange(out.reshape(parts, BLOCK // parts, -1))
    back = back.reshape(parts, BLOCK // parts, 2, 2 * HEAD_DIM).transpose(0, 2, 1, 3).reshape(2 * BLOCK, 2 * HEAD_DIM)
    still = jnp.concatenate([out[:, lanes(1)], out[:, lanes(3)]], axis=0)
    attn = jnp.concatenate([back[:, lanes(0)], jnp.where(moves, back[:, lanes(1)], still)], axis=1)
    mixed = lax.all_gather(attn, "head", axis=1, tiled=True)
    return projection(groups, order, spatial, mixed, weight_cols)


def solution(mesh):
    return jax.shard_map(
        body,
        mesh=mesh,
        in_specs=(P("ctx", "head"), P("ctx", "head"), P("ctx", "head"), P(), P(), P("ctx", "head")),
        out_specs=P("ctx", "head"),
        check_vma=False,
    )
```

```python
import math

import jax
import jax.numpy as jnp
from jax import lax
from jax.experimental import pallas as pl
from jax.experimental.pallas import tpu as pltpu
from jax.sharding import PartitionSpec as P

HEAD_DIM = 128
BLOCK = 512
REACH = 2
BF = jnp.bfloat16
F32 = jnp.float32
RATE = math.log2(math.e) / math.sqrt(HEAD_DIM)
NEAR = ((0, 1, 2, 3, 4, 6), (1, 2, 3, 4, 5, 6))


def lanes(index):
    return slice(index * HEAD_DIM, (index + 1) * HEAD_DIM)


def attention_kernel(heads, bits, q_ref, own_ref, left_ref, right_ref, first_ref, out_ref, s_ref, m_ref, l_ref, acc_ref):
    sides = (left_ref, left_ref, own_ref, own_ref, right_ref, right_ref, first_ref)

    def tile(kind, place, slot):
        if place == 6:
            return first_ref[:, lanes(kind * heads + slot)]
        return sides[place][:, lanes((kind * 2 + place % 2) * heads + slot)]

    for slot in range(heads):
        for b in range(2):
            query = q_ref[:, lanes(b * heads + slot)]
            m_ref[...] = jnp.full_like(m_ref, -jnp.inf)
            l_ref[...] = jnp.zeros_like(l_ref)
            acc_ref[...] = jnp.zeros_like(acc_ref)
            for n, place in enumerate(NEAR[b]):

                @pl.when(bits[b, n] > 0)
                def _():
                    s = lax.dot_general(
                        query, tile(0, place, slot), (((1,), (1,)), ((), ())), preferred_element_type=F32
                    )
                    s_ref[n] = s
                    m = m_ref[...]
                    for c in range(BLOCK // HEAD_DIM):
                        m = jnp.maximum(m, s[:, lanes(c)])
                    m_ref[...] = m

            top = jnp.max(m_ref[...], axis=1, keepdims=True)
            m_ref[...] = jnp.broadcast_to(top, m_ref.shape)
            for n, place in enumerate(NEAR[b]):

                @pl.when(bits[b, n] > 0)
                def _():
                    peak = m_ref[...]
                    total = l_ref[...]
                    parts = []
                    for c in range(BLOCK // HEAD_DIM):
                        w = jnp.exp2((s_ref[n, :, lanes(c)] - peak) * RATE)
                        total = total + w
                        parts.append(w.astype(BF))
                    l_ref[...] = total
                    acc_ref[...] += jnp.dot(
                        jnp.concatenate(parts, axis=1), tile(1, place, slot), preferred_element_type=F32
                    )

            total = jnp.sum(l_ref[...], axis=1, keepdims=True)
            out_ref[:, lanes(b * heads + slot)] = (acc_ref[...] / total).astype(BF)


def attention(heads, bits, query, own, left, right, first):
    vmem = pl.BlockSpec(memory_space=pltpu.VMEM)
    pairs = heads * 2 * 6
    return pl.pallas_call(
        lambda *refs: attention_kernel(heads, *refs),
        out_shape=jax.ShapeDtypeStruct(query.shape, BF),
        in_specs=[pl.BlockSpec(memory_space=pltpu.SMEM)] + [vmem] * 5,
        out_specs=vmem,
        scratch_shapes=[
            pltpu.VMEM((6, BLOCK, BLOCK), F32),
            pltpu.VMEM((BLOCK, HEAD_DIM), F32),
            pltpu.VMEM((BLOCK, HEAD_DIM), F32),
            pltpu.VMEM((BLOCK, HEAD_DIM), F32),
        ],
        compiler_params=pltpu.CompilerParams(vmem_limit_bytes=40 << 20),
        cost_estimate=pl.CostEstimate(
            flops=pairs * 4 * BLOCK * BLOCK * HEAD_DIM,
            bytes_accessed=heads * 16 * BLOCK * HEAD_DIM * 2,
            transcendentals=pairs * BLOCK * BLOCK,
        ),
    )(bits, query, own, left, right, first)


def spatial_kernel(groups, order, spatial_ref, w_ref, part_ref, mixed_w_ref):
    def rows(g, slot):
        return w_ref[pl.ds(pl.multiple_of(order[g * 3 + slot] * HEAD_DIM, HEAD_DIM), HEAD_DIM), :]

    for g in range(groups):
        for slot in range(2):
            mixed_w_ref[(2 * g + slot) * HEAD_DIM : (2 * g + slot + 1) * HEAD_DIM, :] = rows(g, slot)
    chosen = jnp.concatenate([rows(g, 2) for g in range(groups)], axis=0)
    part_ref[...] = jnp.dot(spatial_ref[...], chosen, preferred_element_type=F32)


def spatial_projection(groups, order, spatial, w):
    vmem = pl.BlockSpec(memory_space=pltpu.VMEM)
    return pl.pallas_call(
        lambda *refs: spatial_kernel(groups, *refs),
        out_shape=(
            jax.ShapeDtypeStruct((spatial.shape[0], w.shape[1]), F32),
            jax.ShapeDtypeStruct((groups * 2 * HEAD_DIM, w.shape[1]), BF),
        ),
        in_specs=[pl.BlockSpec(memory_space=pltpu.SMEM)] + [vmem] * 2,
        out_specs=(vmem, vmem),
        compiler_params=pltpu.CompilerParams(vmem_limit_bytes=40 << 20),
    )(order, spatial, w)


def mixed_kernel(part_ref, mixed_ref, w_ref, out_ref):
    out_ref[...] = (part_ref[...] + jnp.dot(mixed_ref[...], w_ref[...], preferred_element_type=F32)).astype(BF)


def mixed_projection(part, mixed, w):
    rows, cols = part.shape
    tile = rows // 4
    return pl.pallas_call(
        mixed_kernel,
        out_shape=jax.ShapeDtypeStruct((rows, cols), BF),
        grid=(rows // tile,),
        in_specs=[
            pl.BlockSpec((tile, cols), lambda i: (i, 0)),
            pl.BlockSpec((tile, mixed.shape[1]), lambda i: (i, 0)),
            pl.BlockSpec(w.shape, lambda i: (0, 0)),
        ],
        out_specs=pl.BlockSpec((tile, cols), lambda i: (i, 0)),
        compiler_params=pltpu.CompilerParams(vmem_limit_bytes=32 << 20),
    )(part, mixed, w)


def slots_of(labels):
    temporal = labels == 1
    a = jnp.where(temporal[:, 0], 0, jnp.where(temporal[:, 1], 1, 2))
    c = jnp.where(~temporal[:, 2], 2, jnp.where(~temporal[:, 1], 1, 0))
    return jnp.stack([a, 3 - a - c, c], axis=1).astype(jnp.int32)


def split_blocks(x):
    return jnp.concatenate([x[:BLOCK], x[BLOCK:]], axis=1)


def position_pack(x, parts):
    rows = x.shape[0] // parts // 2
    return x.reshape(parts, 2, rows, x.shape[1]).transpose(0, 2, 1, 3).reshape(parts, rows, 2 * x.shape[1])


def exchange(x):
    return lax.all_to_all(x, "ctx", 0, 0, tiled=True)


def both_ways(x, count):
    left = lax.ppermute(x, "ctx", [(i, i + 1) for i in range(count - 1)])
    right = lax.ppermute(x, "ctx", [(i + 1, i) for i in range(count - 1)])
    return left, right


def scattered(x, place, steps):
    count = lax.axis_size("ctx")
    reach = count
    for step in steps:
        half = x.shape[0] // 2
        got = lax.ppermute(x[half:], "ctx", [(i, i + step) for i in range(0, count, reach)])
        x = jnp.where(place % reach == step, got, x[:half])
        reach = step
    return x


def body(queries, keys, values, block_mask, head_labels, w_out):
    parts = lax.axis_size("ctx")
    groups = lax.axis_size("head")
    place = lax.axis_index("ctx")
    group = lax.axis_index("head")
    deep = parts // 4
    along_z = [[y * deep + z for z in range(deep)] for y in range(4)]
    along_y = [[y * deep + z for y in range(4)] for z in range(deep)]
    slots = slots_of(head_labels.reshape(groups, 3))
    mine = lax.dynamic_slice_in_dim(slots, group, 1, 0)[0]
    labels = lax.dynamic_slice_in_dim(head_labels, group * 3, 3)
    moves = lax.dynamic_slice_in_dim(labels, mine[1], 1)[0] == 1
    order = (slots + 3 * jnp.arange(groups, dtype=jnp.int32)[:, None]).reshape(-1)

    def head_of(x, slot):
        return lax.dynamic_slice_in_dim(x, mine[slot] * HEAD_DIM, HEAD_DIM, 1)

    q0, q1, q2 = (head_of(queries, s) for s in range(3))
    k0, k1, k2 = (head_of(keys, s) for s in range(3))
    v0, v1, v2 = (head_of(values, s) for s in range(3))

    index = place * 2 + jnp.arange(2, dtype=jnp.int32)
    total_blocks = block_mask.shape[0]
    rows = lax.dynamic_slice_in_dim(block_mask, place * 2, 2, 0)
    cand = index[:, None] + jnp.arange(-REACH, REACH + 1, dtype=jnp.int32)[None, :]
    every = jnp.arange(total_blocks, dtype=jnp.int32)
    hits = jnp.any((cand[:, :, None] == every[None, None, :]) & (rows[:, None, :] == 1), axis=2)
    first_bit = (index > REACH) & (rows[:, 0] == 1)
    bits = jnp.concatenate([hits, first_bit[:, None]], axis=1).astype(jnp.int32)

    shares = scattered(jnp.concatenate([k1, k2, v1, v2], axis=1)[:BLOCK], place, (2 * deep, deep, deep // 2, deep // 4))

    packs = [position_pack(jnp.concatenate(pair, axis=1), parts) for pair in ((q0, q1), (k0, k1), (v0, v1))]
    w_rows = w_out.shape[0] * w_out.shape[1] // HEAD_DIM
    near = BLOCK // parts
    share = shares.shape[0]
    sent = jnp.concatenate(
        [w_out[:, lanes(c)] for c in range(w_out.shape[1] // HEAD_DIM)]
        + [x[:near] for x in (k0, k1, v0, v1)]
        + [shares[:, lanes(c)] for c in range(4)],
        axis=0,
    )
    packed, sent = lax.optimization_barrier((jnp.concatenate(packs, axis=2), sent))
    moved = exchange(packed).reshape(BLOCK, -1)
    moved_q, moved_kv = moved[:, : 4 * HEAD_DIM], moved[:, 4 * HEAD_DIM :]
    rows_z = lax.all_gather(sent, "ctx", axis=0, axis_index_groups=along_z)
    w_z = rows_z[:, :w_rows].reshape(deep, -1, w_out.shape[0], HEAD_DIM)
    w_z = w_z.transpose(0, 2, 1, 3).reshape(deep * w_out.shape[0], -1)
    weight_cols = lax.all_gather(w_z, "ctx", axis=0, axis_index_groups=along_y, tiled=True)
    moving = [rows_z[:, w_rows + n * near : w_rows + (n + 1) * near].reshape(-1, HEAD_DIM) for n in range(4)]
    base = w_rows + 4 * near
    still = [rows_z[:: deep // 4, base + n * share : base + (n + 1) * share].reshape(-1, HEAD_DIM) for n in range(4)]
    quarter = jnp.concatenate(
        [
            moving[0],
            jnp.where(moves, moving[1], still[0]),
            moving[2],
            jnp.where(moves, moving[3], still[2]),
            still[1],
            still[3],
        ],
        axis=1,
    )
    others = [lax.ppermute(quarter, "ctx", [(i, i ^ (deep * k)) for i in range(parts)]) for k in (1, 2, 3)]
    first = jnp.concatenate([quarter] + others, axis=0)

    own2 = jnp.concatenate([split_blocks(k2), split_blocks(v2)], axis=1)
    left2, right2 = both_ways(own2, parts)
    out2 = attention(1, bits, split_blocks(q2), own2, left2, right2, first[:, 4 * HEAD_DIM :])
    attn2 = jnp.concatenate([out2[:, lanes(0)], out2[:, lanes(1)]], axis=0)
    spatial = lax.all_gather(attn2, "head", axis=1, tiled=True)

    def mix(moved, still, kinds):
        cols = []
        for n in range(kinds * 2):
            cols.append(moved[:, lanes(2 * n)])
            cols.append(jnp.where(moves, moved[:, lanes(2 * n + 1)], still[:, lanes(n)]))
        return jnp.concatenate(cols, axis=1)

    own = mix(moved_kv, jnp.concatenate([split_blocks(k1), split_blocks(v1)], axis=1), 2)
    left, right = both_ways(own, parts)
    query = mix(moved_q, split_blocks(q1), 1)
    out = attention(2, bits, query, own, left, right, first[:, : 4 * HEAD_DIM])

    back = exchange(out.reshape(parts, BLOCK // parts, -1))
    back = back.reshape(parts, BLOCK // parts, 2, 2 * HEAD_DIM).transpose(0, 2, 1, 3).reshape(2 * BLOCK, 2 * HEAD_DIM)
    still = jnp.concatenate([out[:, lanes(1)], out[:, lanes(3)]], axis=0)
    attn = jnp.concatenate([back[:, lanes(0)], jnp.where(moves, back[:, lanes(1)], still)], axis=1)
    mixed = lax.all_gather(attn, "head", axis=1, tiled=True)
    part, mixed_w = spatial_projection(groups, order, spatial, weight_cols)
    return mixed_projection(part, mixed, mixed_w)


def solution(mesh):
    return jax.shard_map(
        body,
        mesh=mesh,
        in_specs=(P("ctx", "head"), P("ctx", "head"), P("ctx", "head"), P(), P(), P("ctx", "head")),
        out_specs=P("ctx", "head"),
        check_vma=False,
    )
```

```python
import math

import jax
import jax.numpy as jnp
from jax import lax
from jax.experimental import pallas as pl
from jax.experimental.pallas import tpu as pltpu
from jax.sharding import PartitionSpec as P

HEAD_DIM = 128
BLOCK = 512
REACH = 2
BF = jnp.bfloat16
F32 = jnp.float32
RATE = math.log2(math.e) / math.sqrt(HEAD_DIM)
SPAN = 2 * REACH + 1


def lanes(index):
    return slice(index * HEAD_DIM, (index + 1) * HEAD_DIM)


VMEM = pl.BlockSpec(memory_space=pltpu.VMEM)
SMEM = pl.BlockSpec(memory_space=pltpu.SMEM)


def near_kernel(heads, bits, q_ref, own_ref, left_ref, right_ref, acc_ref, stat_ref, s_ref, m_ref, l_ref):
    sides = (left_ref, left_ref, own_ref, own_ref, right_ref, right_ref)

    def tile(kind, place, slot):
        return sides[place][:, lanes((kind * 2 + place % 2) * heads + slot)]

    for slot in range(heads):
        for b in range(2):
            here = lanes(b * heads + slot)
            query = q_ref[:, here]
            m_ref[...] = jnp.full_like(m_ref, -jnp.inf)
            l_ref[...] = jnp.zeros_like(l_ref)
            acc_ref[:, here] = jnp.zeros_like(m_ref)
            for n in range(SPAN):

                @pl.when(bits[b, n] > 0)
                def _():
                    s = lax.dot_general(
                        query, tile(0, b + n, slot), (((1,), (1,)), ((), ())), preferred_element_type=F32
                    )
                    s_ref[n] = s
                    m = m_ref[...]
                    for c in range(BLOCK // HEAD_DIM):
                        m = jnp.maximum(m, s[:, lanes(c)])
                    m_ref[...] = m

            m_ref[...] = jnp.broadcast_to(jnp.max(m_ref[...], axis=1, keepdims=True), m_ref.shape)
            for n in range(SPAN):

                @pl.when(bits[b, n] > 0)
                def _():
                    peak = m_ref[...]
                    total = l_ref[...]
                    parts = []
                    for c in range(BLOCK // HEAD_DIM):
                        w = jnp.exp2((s_ref[n, :, lanes(c)] - peak) * RATE)
                        total = total + w
                        parts.append(w.astype(BF))
                    l_ref[...] = total
                    acc_ref[:, here] += jnp.dot(
                        jnp.concatenate(parts, axis=1), tile(1, b + n, slot), preferred_element_type=F32
                    )

            total = jnp.sum(l_ref[...], axis=1, keepdims=True)
            lane = lax.broadcasted_iota(jnp.int32, m_ref.shape, 1)
            stat_ref[:, here] = jnp.where(lane < HEAD_DIM // 2, m_ref[...], total)


def near_attention(heads, bits, query, own, left, right):
    state = jax.ShapeDtypeStruct(query.shape, F32)
    pairs = heads * 2 * SPAN
    return pl.pallas_call(
        lambda *refs: near_kernel(heads, *refs),
        out_shape=(state, state),
        in_specs=[SMEM] + [VMEM] * 4,
        out_specs=(VMEM, VMEM),
        scratch_shapes=[
            pltpu.VMEM((SPAN, BLOCK, BLOCK), F32),
            pltpu.VMEM((BLOCK, HEAD_DIM), F32),
            pltpu.VMEM((BLOCK, HEAD_DIM), F32),
        ],
        compiler_params=pltpu.CompilerParams(vmem_limit_bytes=32 << 20),
        cost_estimate=pl.CostEstimate(
            flops=pairs * 4 * BLOCK * BLOCK * HEAD_DIM,
            bytes_accessed=heads * 16 * BLOCK * HEAD_DIM * 2,
            transcendentals=pairs * BLOCK * BLOCK,
        ),
    )(bits, query, own, left, right)


def first_kernel(bits, qm_ref, am_ref, sm_ref, qs_ref, as_ref, ss_ref, f0, f1, f2, f3, outm_ref, outs_ref):
    quarters = (f0, f1, f2, f3)

    def block(column):
        return jnp.concatenate([f[:, lanes(column)] for f in quarters], axis=0)

    for slot in range(3):
        heads = 1 if slot == 2 else 2
        q_ref, acc_ref, stat_ref, out_ref = (
            (qs_ref, as_ref, ss_ref, outs_ref) if slot == 2 else (qm_ref, am_ref, sm_ref, outm_ref)
        )
        key, val = ((0, 2), (1, 3), (4, 5))[slot]
        for b in range(2):
            here = lanes(b * heads + slot % 2)
            start = here.start
            total = stat_ref[:, start + HEAD_DIM - 1 : start + HEAD_DIM]

            @pl.when(bits[b, SPAN] > 0)
            def _():
                peak = stat_ref[:, start : start + 1]
                s = lax.dot_general(q_ref[:, here], block(key), (((1,), (1,)), ((), ())), preferred_element_type=F32)
                top = jnp.maximum(peak, jnp.max(s, axis=1, keepdims=True))
                keep = jnp.exp2((peak - top) * RATE)
                w = jnp.exp2((s - top) * RATE)
                mixed = acc_ref[:, here] * keep + jnp.dot(w.astype(BF), block(val), preferred_element_type=F32)
                out_ref[:, here] = (mixed / (total * keep + jnp.sum(w, axis=1, keepdims=True))).astype(BF)

            @pl.when(bits[b, SPAN] <= 0)
            def _():
                out_ref[:, here] = (acc_ref[:, here] / total).astype(BF)


def first_attention(bits, mixed, spatial, first):
    pairs = 6
    return pl.pallas_call(
        first_kernel,
        out_shape=(jax.ShapeDtypeStruct(mixed[0].shape, BF), jax.ShapeDtypeStruct(spatial[0].shape, BF)),
        in_specs=[SMEM] + [VMEM] * 10,
        out_specs=(VMEM, VMEM),
        compiler_params=pltpu.CompilerParams(vmem_limit_bytes=32 << 20),
        cost_estimate=pl.CostEstimate(
            flops=pairs * 4 * BLOCK * BLOCK * HEAD_DIM,
            bytes_accessed=pairs * 8 * BLOCK * HEAD_DIM * 2,
            transcendentals=pairs * BLOCK * BLOCK,
        ),
    )(bits, *mixed, *spatial, *first)


def unpack_kernel(moves, x_ref, quarter_ref, w_ref):
    deep = x_ref.shape[0]
    blocks = w_ref.shape[1] // HEAD_DIM
    rows = w_ref.shape[0] // deep
    base = blocks * rows
    near = BLOCK // 4 // deep
    share = BLOCK // 16
    for z in range(deep):
        for c in range(blocks):
            w_ref[z * rows : (z + 1) * rows, lanes(c)] = x_ref[z, c * rows : (c + 1) * rows, :]
    pairs = [x_ref[z, base : base + 4 * near, :].astype(F32) for z in range(deep)]
    moving = [
        jnp.concatenate([pair[n * near : (n + 1) * near] for pair in pairs], axis=0).astype(BF) for n in range(4)
    ]
    base += 4 * near
    still = [
        jnp.concatenate(
            [x_ref[z, base + n * share : base + (n + 1) * share, :] for z in range(0, deep, deep // 4)], axis=0
        )
        for n in range(4)
    ]
    flag = moves[0] > 0
    quarter_ref[:, lanes(0)] = moving[0]
    quarter_ref[:, lanes(2)] = moving[2]
    quarter_ref[:, lanes(4)] = still[1]
    quarter_ref[:, lanes(5)] = still[3]
    quarter_ref[:, lanes(1)] = jnp.where(flag, moving[1].astype(F32), still[0].astype(F32)).astype(BF)
    quarter_ref[:, lanes(3)] = jnp.where(flag, moving[3].astype(F32), still[2].astype(F32)).astype(BF)


def unpack(moves, x, w_rows, w_cols):
    return pl.pallas_call(
        unpack_kernel,
        out_shape=(
            jax.ShapeDtypeStruct((BLOCK // 4, 6 * HEAD_DIM), BF),
            jax.ShapeDtypeStruct((w_rows, w_cols), BF),
        ),
        in_specs=[SMEM, VMEM],
        out_specs=(VMEM, VMEM),
        compiler_params=pltpu.CompilerParams(vmem_limit_bytes=16 << 20),
    )(moves.astype(jnp.int32).reshape(1), x)


def spatial_kernel(groups, order, spatial_ref, w0, w1, w2, w3, part_ref, mixed_w_ref, w_ref):
    quarter = w0.shape[0]
    for k, w in enumerate((w0, w1, w2, w3)):
        at = jnp.bitwise_xor(order[groups * 3], k) * quarter
        w_ref[pl.ds(pl.multiple_of(at, HEAD_DIM), quarter), :] = w[...]

    def rows(g, slot):
        return w_ref[pl.ds(pl.multiple_of(order[g * 3 + slot] * HEAD_DIM, HEAD_DIM), HEAD_DIM), :]

    for g in range(groups):
        for slot in range(2):
            mixed_w_ref[(2 * g + slot) * HEAD_DIM : (2 * g + slot + 1) * HEAD_DIM, :] = rows(g, slot)
    chosen = jnp.concatenate([rows(g, 2) for g in range(groups)], axis=0)
    part_ref[...] = jnp.dot(spatial_ref[...], chosen, preferred_element_type=F32)


def spatial_projection(groups, order, spatial, w):
    rows, cols = w[0].shape
    return pl.pallas_call(
        lambda *refs: spatial_kernel(groups, *refs),
        out_shape=(
            jax.ShapeDtypeStruct((spatial.shape[0], cols), F32),
            jax.ShapeDtypeStruct((groups * 2 * HEAD_DIM, cols), BF),
        ),
        in_specs=[SMEM] + [VMEM] * 5,
        out_specs=(VMEM, VMEM),
        scratch_shapes=[pltpu.VMEM((4 * rows, cols), BF)],
        compiler_params=pltpu.CompilerParams(vmem_limit_bytes=32 << 20),
    )(order, spatial, *w)


def mixed_kernel(part_ref, mixed_ref, w_ref, out_ref):
    out_ref[...] = (part_ref[...] + jnp.dot(mixed_ref[...], w_ref[...], preferred_element_type=F32)).astype(BF)


def mixed_projection(part, mixed, w):
    rows, cols = part.shape
    tile = rows // 4
    return pl.pallas_call(
        mixed_kernel,
        out_shape=jax.ShapeDtypeStruct((rows, cols), BF),
        grid=(rows // tile,),
        in_specs=[
            pl.BlockSpec((tile, cols), lambda i: (i, 0)),
            pl.BlockSpec((tile, mixed.shape[1]), lambda i: (i, 0)),
            pl.BlockSpec(w.shape, lambda i: (0, 0)),
        ],
        out_specs=pl.BlockSpec((tile, cols), lambda i: (i, 0)),
        compiler_params=pltpu.CompilerParams(vmem_limit_bytes=32 << 20),
    )(part, mixed, w)


def slots_of(labels):
    temporal = labels == 1
    a = jnp.where(temporal[:, 0], 0, jnp.where(temporal[:, 1], 1, 2))
    c = jnp.where(~temporal[:, 2], 2, jnp.where(~temporal[:, 1], 1, 0))
    return jnp.stack([a, 3 - a - c, c], axis=1).astype(jnp.int32)


def split_blocks(x):
    return jnp.concatenate([x[:BLOCK], x[BLOCK:]], axis=1)


def position_pack(x, parts):
    rows = x.shape[0] // parts // 2
    return x.reshape(parts, 2, rows, x.shape[1]).transpose(0, 2, 1, 3).reshape(parts, rows, 2 * x.shape[1])


def exchange(x):
    return lax.all_to_all(x, "ctx", 0, 0, tiled=True)


def both_ways(x, count):
    left = lax.ppermute(x, "ctx", [(i, i + 1) for i in range(count - 1)])
    right = lax.ppermute(x, "ctx", [(i + 1, i) for i in range(count - 1)])
    return left, right


def scattered(x, place, steps):
    count = lax.axis_size("ctx")
    reach = count
    for step in steps:
        half = x.shape[0] // 2
        got = lax.ppermute(x[half:], "ctx", [(i, i + step) for i in range(0, count, reach)])
        x = jnp.where(place % reach == step, got, x[:half])
        reach = step
    return x


def body(queries, keys, values, block_mask, head_labels, w_out):
    parts = lax.axis_size("ctx")
    groups = lax.axis_size("head")
    place = lax.axis_index("ctx")
    group = lax.axis_index("head")
    deep = parts // 4
    along_z = [[y * deep + z for z in range(deep)] for y in range(4)]
    slots = slots_of(head_labels.reshape(groups, 3))
    mine = lax.dynamic_slice_in_dim(slots, group, 1, 0)[0]
    labels = lax.dynamic_slice_in_dim(head_labels, group * 3, 3)
    moves = lax.dynamic_slice_in_dim(labels, mine[1], 1)[0] == 1
    order = (slots + 3 * jnp.arange(groups, dtype=jnp.int32)[:, None]).reshape(-1)
    order = jnp.concatenate([order, (place // deep)[None].astype(jnp.int32)])

    def head_of(x, slot):
        return lax.dynamic_slice_in_dim(x, mine[slot] * HEAD_DIM, HEAD_DIM, 1)

    q0, q1, q2 = (head_of(queries, s) for s in range(3))
    k0, k1, k2 = (head_of(keys, s) for s in range(3))
    v0, v1, v2 = (head_of(values, s) for s in range(3))

    index = place * 2 + jnp.arange(2, dtype=jnp.int32)
    total_blocks = block_mask.shape[0]
    rows = lax.dynamic_slice_in_dim(block_mask, place * 2, 2, 0)
    cand = index[:, None] + jnp.arange(-REACH, REACH + 1, dtype=jnp.int32)[None, :]
    every = jnp.arange(total_blocks, dtype=jnp.int32)
    hits = jnp.any((cand[:, :, None] == every[None, None, :]) & (rows[:, None, :] == 1), axis=2)
    first_bit = (index > REACH) & (rows[:, 0] == 1)
    bits = jnp.concatenate([hits, first_bit[:, None]], axis=1).astype(jnp.int32)

    own2 = jnp.concatenate([split_blocks(k2), split_blocks(v2)], axis=1)
    left2, right2 = both_ways(own2, parts)

    shares = scattered(jnp.concatenate([k1, k2, v1, v2], axis=1)[:BLOCK], place, (2 * deep, deep, deep // 2, deep // 4))

    packs = [position_pack(jnp.concatenate(pair, axis=1), parts) for pair in ((q0, q1), (k0, k1), (v0, v1))]
    near = BLOCK // parts
    sent = jnp.concatenate(
        [w_out[:, lanes(c)] for c in range(w_out.shape[1] // HEAD_DIM)]
        + [x[:near] for x in (k0, k1, v0, v1)]
        + [shares[:, lanes(c)] for c in range(4)],
        axis=0,
    )
    packed, sent, left2, right2 = lax.optimization_barrier((jnp.concatenate(packs, axis=2), sent, left2, right2))
    moved = exchange(packed).reshape(BLOCK, -1)
    moved_q, moved_kv = moved[:, : 4 * HEAD_DIM], moved[:, 4 * HEAD_DIM :]
    rows_z = lax.all_gather(sent, "ctx", axis=0, axis_index_groups=along_z)
    def mix(moved, still, kinds):
        cols = []
        for n in range(kinds * 2):
            cols.append(moved[:, lanes(2 * n)])
            cols.append(jnp.where(moves, moved[:, lanes(2 * n + 1)], still[:, lanes(n)]))
        return jnp.concatenate(cols, axis=1)

    own = mix(moved_kv, jnp.concatenate([split_blocks(k1), split_blocks(v1)], axis=1), 2)
    left, right = both_ways(own, parts)
    query = mix(moved_q, split_blocks(q1), 1)
    left, right, rows_z = lax.optimization_barrier((left, right, rows_z))
    quarter, w_z = unpack(moves, rows_z, deep * w_out.shape[0], w_out.shape[1])

    def along_y(x):
        return [lax.ppermute(x, "ctx", [(i, i ^ (deep * k)) for i in range(parts)]) for k in (1, 2, 3)]

    first = [quarter] + along_y(quarter)
    w_z, first = lax.optimization_barrier((w_z, first))
    w_parts = [w_z] + along_y(w_z)

    query2 = split_blocks(q2)
    spatial = near_attention(1, bits, query2, own2, left2, right2)
    mixed = near_attention(2, bits, query, own, left, right)
    out, out2 = first_attention(bits, (query, *mixed), (query2, *spatial), first)
    attn2 = jnp.concatenate([out2[:, lanes(0)], out2[:, lanes(1)]], axis=0)
    spatial = lax.all_gather(attn2, "head", axis=1, tiled=True)

    back = exchange(out.reshape(parts, BLOCK // parts, -1))
    back = back.reshape(parts, BLOCK // parts, 2, 2 * HEAD_DIM).transpose(0, 2, 1, 3).reshape(2 * BLOCK, 2 * HEAD_DIM)
    still = jnp.concatenate([out[:, lanes(1)], out[:, lanes(3)]], axis=0)
    attn = jnp.concatenate([back[:, lanes(0)], jnp.where(moves, back[:, lanes(1)], still)], axis=1)
    mixed = lax.all_gather(attn, "head", axis=1, tiled=True)
    part, mixed_w = spatial_projection(groups, order, spatial, w_parts)
    return mixed_projection(part, mixed, mixed_w)


def solution(mesh):
    return jax.shard_map(
        body,
        mesh=mesh,
        in_specs=(P("ctx", "head"), P("ctx", "head"), P("ctx", "head"), P(), P(), P("ctx", "head")),
        out_specs=P("ctx", "head"),
        check_vma=False,
    )
```

```python
import math

import jax
import jax.numpy as jnp
from jax import lax
from jax.experimental import pallas as pl
from jax.experimental.pallas import tpu as pltpu
from jax.sharding import PartitionSpec as P

HEAD_DIM = 128
BLOCK = 512
REACH = 2
BF = jnp.bfloat16
F32 = jnp.float32
RATE = math.log2(math.e) / math.sqrt(HEAD_DIM)
SPAN = 2 * REACH + 1
COVER = 1 << 35


def lanes(index):
    return slice(index * HEAD_DIM, (index + 1) * HEAD_DIM)


VMEM = pl.BlockSpec(memory_space=pltpu.VMEM)
SMEM = pl.BlockSpec(memory_space=pltpu.SMEM)


def near_kernel(heads, bits, q_ref, own_ref, left_ref, right_ref, acc_ref, stat_ref, s_ref, m_ref, l_ref):
    sides = (left_ref, left_ref, own_ref, own_ref, right_ref, right_ref)

    def tile(kind, place, slot):
        return sides[place][:, lanes((kind * 2 + place % 2) * heads + slot)]

    for slot in range(heads):
        for b in range(2):
            here = lanes(b * heads + slot)
            query = q_ref[:, here]
            m_ref[...] = jnp.full_like(m_ref, -jnp.inf)
            l_ref[...] = jnp.zeros_like(l_ref)
            acc_ref[:, here] = jnp.zeros_like(m_ref)
            for n in range(SPAN):

                @pl.when(bits[b, n] > 0)
                def _():
                    s = lax.dot_general(
                        query, tile(0, b + n, slot), (((1,), (1,)), ((), ())), preferred_element_type=F32
                    )
                    s_ref[n] = s
                    m = m_ref[...]
                    for c in range(BLOCK // HEAD_DIM):
                        m = jnp.maximum(m, s[:, lanes(c)])
                    m_ref[...] = m

            m_ref[...] = jnp.broadcast_to(jnp.max(m_ref[...], axis=1, keepdims=True), m_ref.shape)
            for n in range(SPAN):

                @pl.when(bits[b, n] > 0)
                def _():
                    peak = m_ref[...]
                    total = l_ref[...]
                    parts = []
                    for c in range(BLOCK // HEAD_DIM):
                        w = jnp.exp2((s_ref[n, :, lanes(c)] - peak) * RATE)
                        total = total + w
                        parts.append(w.astype(BF))
                    l_ref[...] = total
                    acc_ref[:, here] += jnp.dot(
                        jnp.concatenate(parts, axis=1), tile(1, b + n, slot), preferred_element_type=F32
                    )

            total = jnp.sum(l_ref[...], axis=1, keepdims=True)
            lane = lax.broadcasted_iota(jnp.int32, m_ref.shape, 1)
            stat_ref[:, here] = jnp.where(lane < HEAD_DIM // 2, m_ref[...], total)


def near_attention(heads, bits, query, own, left, right):
    state = jax.ShapeDtypeStruct(query.shape, F32)
    pairs = heads * 2 * SPAN
    return pl.pallas_call(
        lambda *refs: near_kernel(heads, *refs),
        out_shape=(state, state),
        in_specs=[SMEM] + [VMEM] * 4,
        out_specs=(VMEM, VMEM),
        scratch_shapes=[
            pltpu.VMEM((SPAN, BLOCK, BLOCK), F32),
            pltpu.VMEM((BLOCK, HEAD_DIM), F32),
            pltpu.VMEM((BLOCK, HEAD_DIM), F32),
        ],
        compiler_params=pltpu.CompilerParams(vmem_limit_bytes=32 << 20),
        cost_estimate=pl.CostEstimate(
            flops=pairs * 4 * BLOCK * BLOCK * HEAD_DIM,
            bytes_accessed=heads * 16 * BLOCK * HEAD_DIM * 2,
            transcendentals=pairs * BLOCK * BLOCK,
        ),
    )(bits, query, own, left, right)


def first_kernel(bits, qm_ref, am_ref, sm_ref, qs_ref, as_ref, ss_ref, f0, f1, f2, f3, outm_ref, outs_ref):
    quarters = (f0, f1, f2, f3)

    def block(column):
        return jnp.concatenate([f[:, lanes(column)] for f in quarters], axis=0)

    for slot in range(3):
        heads = 1 if slot == 2 else 2
        q_ref, acc_ref, stat_ref, out_ref = (
            (qs_ref, as_ref, ss_ref, outs_ref) if slot == 2 else (qm_ref, am_ref, sm_ref, outm_ref)
        )
        key, val = ((0, 2), (1, 3), (4, 5))[slot]
        for b in range(2):
            here = lanes(b * heads + slot % 2)
            start = here.start
            total = stat_ref[:, start + HEAD_DIM - 1 : start + HEAD_DIM]

            @pl.when(bits[b, SPAN] > 0)
            def _():
                peak = stat_ref[:, start : start + 1]
                s = lax.dot_general(q_ref[:, here], block(key), (((1,), (1,)), ((), ())), preferred_element_type=F32)
                top = jnp.maximum(peak, jnp.max(s, axis=1, keepdims=True))
                keep = jnp.exp2((peak - top) * RATE)
                w = jnp.exp2((s - top) * RATE)
                mixed = acc_ref[:, here] * keep + jnp.dot(w.astype(BF), block(val), preferred_element_type=F32)
                out_ref[:, here] = (mixed / (total * keep + jnp.sum(w, axis=1, keepdims=True))).astype(BF)

            @pl.when(bits[b, SPAN] <= 0)
            def _():
                out_ref[:, here] = (acc_ref[:, here] / total).astype(BF)


def first_attention(bits, mixed, spatial, first):
    pairs = 6
    return pl.pallas_call(
        first_kernel,
        out_shape=(jax.ShapeDtypeStruct(mixed[0].shape, BF), jax.ShapeDtypeStruct(spatial[0].shape, BF)),
        in_specs=[SMEM] + [VMEM] * 10,
        out_specs=(VMEM, VMEM),
        compiler_params=pltpu.CompilerParams(vmem_limit_bytes=32 << 20),
        cost_estimate=pl.CostEstimate(
            flops=pairs * 4 * BLOCK * BLOCK * HEAD_DIM,
            bytes_accessed=pairs * 8 * BLOCK * HEAD_DIM * 2,
            transcendentals=pairs * BLOCK * BLOCK,
        ),
    )(bits, *mixed, *spatial, *first)


def mix_kernel(moves, moved_ref, q1_ref, k1_ref, v1_ref, query_ref, own_ref):
    kept = (q1_ref, k1_ref, v1_ref)

    def target(n):
        return (query_ref, lanes(n)) if n < 4 else (own_ref, lanes(n - 4))

    for n in range(12):
        out_ref, here = target(n)
        if n % 2 == 0:
            out_ref[:, here] = moved_ref[:, lanes(n)]

    @pl.when(moves[0] > 0)
    def _():
        for n in range(1, 12, 2):
            out_ref, here = target(n)
            out_ref[:, here] = moved_ref[:, lanes(n)]

    @pl.when(moves[0] <= 0)
    def _():
        for n in range(1, 12, 2):
            out_ref, here = target(n)
            b = n // 2 % 2
            out_ref[:, here] = kept[n // 4][b * BLOCK : (b + 1) * BLOCK, :]


def mix(moves, moved, kept):
    return pl.pallas_call(
        mix_kernel,
        out_shape=(
            jax.ShapeDtypeStruct((BLOCK, 4 * HEAD_DIM), BF),
            jax.ShapeDtypeStruct((BLOCK, 8 * HEAD_DIM), BF),
        ),
        in_specs=[SMEM] + [VMEM] * 4,
        out_specs=(VMEM, VMEM),
        compiler_params=pltpu.CompilerParams(vmem_limit_bytes=16 << 20),
    )(moves, moved, *kept)


def unpack_kernel(moves, x_ref, quarter_ref, w_ref):
    deep = x_ref.shape[0]
    blocks = w_ref.shape[1] // HEAD_DIM
    rows = w_ref.shape[0] // deep
    base = blocks * rows
    near = BLOCK // 4 // deep
    share = BLOCK // 16
    for z in range(deep):
        for c in range(blocks):
            w_ref[z * rows : (z + 1) * rows, lanes(c)] = x_ref[z, c * rows : (c + 1) * rows, :]
    pairs = [x_ref[z, base : base + 4 * near, :].astype(F32) for z in range(deep)]
    moving = [
        jnp.concatenate([pair[n * near : (n + 1) * near] for pair in pairs], axis=0).astype(BF) for n in range(4)
    ]
    base += 4 * near
    still = [
        jnp.concatenate(
            [x_ref[z, base + n * share : base + (n + 1) * share, :] for z in range(0, deep, deep // 4)], axis=0
        )
        for n in range(4)
    ]
    flag = moves[0] > 0
    quarter_ref[:, lanes(0)] = moving[0]
    quarter_ref[:, lanes(2)] = moving[2]
    quarter_ref[:, lanes(4)] = still[1]
    quarter_ref[:, lanes(5)] = still[3]
    quarter_ref[:, lanes(1)] = jnp.where(flag, moving[1].astype(F32), still[0].astype(F32)).astype(BF)
    quarter_ref[:, lanes(3)] = jnp.where(flag, moving[3].astype(F32), still[2].astype(F32)).astype(BF)


def unpack(moves, x, w_rows, w_cols):
    return pl.pallas_call(
        unpack_kernel,
        out_shape=(
            jax.ShapeDtypeStruct((BLOCK // 4, 6 * HEAD_DIM), BF),
            jax.ShapeDtypeStruct((w_rows, w_cols), BF),
        ),
        in_specs=[SMEM, VMEM],
        out_specs=(VMEM, VMEM),
        compiler_params=pltpu.CompilerParams(vmem_limit_bytes=16 << 20),
        cost_estimate=pl.CostEstimate(flops=COVER, bytes_accessed=0, transcendentals=0),
    )(moves, x)


def spatial_kernel(groups, order, spatial_ref, w_ref, part_ref, mixed_w_ref):
    def rows(g, slot):
        return w_ref[pl.ds(pl.multiple_of(order[g * 3 + slot] * HEAD_DIM, HEAD_DIM), HEAD_DIM), :]

    for g in range(groups):
        for slot in range(2):
            mixed_w_ref[(2 * g + slot) * HEAD_DIM : (2 * g + slot + 1) * HEAD_DIM, :] = rows(g, slot)
    chosen = jnp.concatenate([rows(g, 2) for g in range(groups)], axis=0)
    part_ref[...] = jnp.dot(spatial_ref[...], chosen, preferred_element_type=F32)


def spatial_projection(groups, order, spatial, w):
    return pl.pallas_call(
        lambda *refs: spatial_kernel(groups, *refs),
        out_shape=(
            jax.ShapeDtypeStruct((spatial.shape[0], w.shape[1]), F32),
            jax.ShapeDtypeStruct((groups * 2 * HEAD_DIM, w.shape[1]), BF),
        ),
        in_specs=[SMEM] + [VMEM] * 2,
        out_specs=(VMEM, VMEM),
        compiler_params=pltpu.CompilerParams(vmem_limit_bytes=32 << 20),
    )(order, spatial, w)


def mixed_kernel(part_ref, mixed_ref, w_ref, out_ref):
    out_ref[...] = (part_ref[...] + jnp.dot(mixed_ref[...], w_ref[...], preferred_element_type=F32)).astype(BF)


def mixed_projection(part, mixed, w):
    rows, cols = part.shape
    tile = rows // 4
    return pl.pallas_call(
        mixed_kernel,
        out_shape=jax.ShapeDtypeStruct((rows, cols), BF),
        grid=(rows // tile,),
        in_specs=[
            pl.BlockSpec((tile, cols), lambda i: (i, 0)),
            pl.BlockSpec((tile, mixed.shape[1]), lambda i: (i, 0)),
            pl.BlockSpec(w.shape, lambda i: (0, 0)),
        ],
        out_specs=pl.BlockSpec((tile, cols), lambda i: (i, 0)),
        compiler_params=pltpu.CompilerParams(vmem_limit_bytes=60 << 20),
    )(part, mixed, w)


def slots_of(labels):
    temporal = labels == 1
    a = jnp.where(temporal[:, 0], 0, jnp.where(temporal[:, 1], 1, 2))
    c = jnp.where(~temporal[:, 2], 2, jnp.where(~temporal[:, 1], 1, 0))
    return jnp.stack([a, 3 - a - c, c], axis=1).astype(jnp.int32)


def split_blocks(x):
    return jnp.concatenate([x[:BLOCK], x[BLOCK:]], axis=1)


def position_pack(x, parts):
    rows = x.shape[0] // parts // 2
    return x.reshape(parts, 2, rows, x.shape[1]).transpose(0, 2, 1, 3).reshape(parts, rows, 2 * x.shape[1])


def exchange(x):
    return lax.all_to_all(x, "ctx", 0, 0, tiled=True)


def both_ways(x, count):
    left = lax.ppermute(x, "ctx", [(i, i + 1) for i in range(count - 1)])
    right = lax.ppermute(x, "ctx", [(i + 1, i) for i in range(count - 1)])
    return left, right


def scattered(x, index, unit, live):
    count = lax.axis_size("ctx")
    rows = x.shape[0] // 4
    out = x[:rows]
    for k in (1, 2, 3):
        got = lax.ppermute(x[k * rows : (k + 1) * rows], "ctx", [(i, i + k * unit) for i in range(0, count, live)])
        out = jnp.where(index == k, got, out)
    return out


def body(queries, keys, values, block_mask, head_labels, w_out):
    parts = lax.axis_size("ctx")
    groups = lax.axis_size("head")
    place = lax.axis_index("ctx")
    group = lax.axis_index("head")
    deep = parts // 4
    y_lines = [[y * deep + z for y in range(4)] for z in range(deep)]
    along_z = [[y * deep + z for z in range(deep)] for y in range(4)]
    slots = slots_of(head_labels.reshape(groups, 3))
    mine = lax.dynamic_slice_in_dim(slots, group, 1, 0)[0]
    labels = lax.dynamic_slice_in_dim(head_labels, group * 3, 3)
    moves = lax.dynamic_slice_in_dim(labels, mine[1], 1)
    order = (slots + 3 * jnp.arange(groups, dtype=jnp.int32)[:, None]).reshape(-1)

    def head_of(x, slot):
        return lax.dynamic_slice_in_dim(x, mine[slot] * HEAD_DIM, HEAD_DIM, 1)

    q0, q1, q2 = (head_of(queries, s) for s in range(3))
    k0, k1, k2 = (head_of(keys, s) for s in range(3))
    v0, v1, v2 = (head_of(values, s) for s in range(3))

    index = place * 2 + jnp.arange(2, dtype=jnp.int32)
    total_blocks = block_mask.shape[0]
    rows = lax.dynamic_slice_in_dim(block_mask, place * 2, 2, 0)
    cand = index[:, None] + jnp.arange(-REACH, REACH + 1, dtype=jnp.int32)[None, :]
    every = jnp.arange(total_blocks, dtype=jnp.int32)
    hits = jnp.any((cand[:, :, None] == every[None, None, :]) & (rows[:, None, :] == 1), axis=2)
    first_bit = (index > REACH) & (rows[:, 0] == 1)
    bits = jnp.concatenate([hits, first_bit[:, None]], axis=1).astype(jnp.int32)

    shares = jnp.concatenate([k1, k2, v1, v2], axis=1)[:BLOCK]
    shares = scattered(shares, place // deep, deep, parts)
    shares = scattered(shares, place % deep // (deep // 4), deep // 4, deep)

    packs = [position_pack(jnp.concatenate(pair, axis=1), parts) for pair in ((q0, q1), (k0, k1), (v0, v1))]
    near = BLOCK // parts
    sent = jnp.concatenate(
        [w_out[:, lanes(c)] for c in range(w_out.shape[1] // HEAD_DIM)]
        + [x[:near] for x in (k0, k1, v0, v1)]
        + [shares[:, lanes(c)] for c in range(4)],
        axis=0,
    )
    own2 = jnp.concatenate([split_blocks(k2), split_blocks(v2)], axis=1)
    packed, sent = lax.optimization_barrier((jnp.concatenate(packs, axis=2), sent))
    moved = exchange(packed).reshape(BLOCK, -1)
    rows_z = lax.all_gather(sent, "ctx", axis=0, axis_index_groups=along_z)
    quarter, w_z = unpack(moves, rows_z, deep * w_out.shape[0], w_out.shape[1])
    moved, quarter = lax.optimization_barrier((moved, quarter))
    query, own = mix(moves, moved, (q1, k1, v1))
    left, right = both_ways(own, parts)

    def along_y(x):
        return [lax.ppermute(x, "ctx", [(i, i ^ (deep * k)) for i in range(parts)]) for k in (1, 2, 3)]

    first = [quarter] + along_y(quarter)
    left, right, first = lax.optimization_barrier((left, right, first))
    w = lax.all_gather(w_z, "ctx", axis=0, axis_index_groups=y_lines, tiled=True)

    mixed = near_attention(2, bits, query, own, left, right)
    own2, _, _ = lax.optimization_barrier((own2, left, right))
    query2 = split_blocks(q2)
    spatial = near_attention(1, bits, query2, own2, *both_ways(own2, parts))
    out, out2 = first_attention(bits, (query, *mixed), (query2, *spatial), first)
    attn2 = jnp.concatenate([out2[:, lanes(0)], out2[:, lanes(1)]], axis=0)
    spatial = lax.all_gather(attn2, "head", axis=1, tiled=True)

    back = exchange(out.reshape(parts, BLOCK // parts, -1))
    back = back.reshape(parts, BLOCK // parts, 2, 2 * HEAD_DIM).transpose(0, 2, 1, 3).reshape(2 * BLOCK, 2 * HEAD_DIM)
    still = jnp.concatenate([out[:, lanes(1)], out[:, lanes(3)]], axis=0)
    attn = jnp.concatenate([back[:, lanes(0)], jnp.where(moves[0] > 0, back[:, lanes(1)], still)], axis=1)
    mixed = lax.all_gather(attn, "head", axis=1, tiled=True)
    part, mixed_w = spatial_projection(groups, order, spatial, w)
    return mixed_projection(part, mixed, mixed_w)


def solution(mesh):
    return jax.shard_map(
        body,
        mesh=mesh,
        in_specs=(P("ctx", "head"), P("ctx", "head"), P("ctx", "head"), P(), P(), P("ctx", "head")),
        out_specs=P("ctx", "head"),
        check_vma=False,
    )
```

```python
import math

import jax
import jax.numpy as jnp
from jax import lax
from jax.experimental import pallas as pl
from jax.experimental.pallas import tpu as pltpu
from jax.sharding import PartitionSpec as P

HEAD_DIM = 128
BLOCK = 512
REACH = 2
BF = jnp.bfloat16
F32 = jnp.float32
RATE = math.log2(math.e) / math.sqrt(HEAD_DIM)
SPAN = 2 * REACH + 1
COVER = 1 << 36


def lanes(index):
    return slice(index * HEAD_DIM, (index + 1) * HEAD_DIM)


VMEM = pl.BlockSpec(memory_space=pltpu.VMEM)
SMEM = pl.BlockSpec(memory_space=pltpu.SMEM)


def attention_kernel(heads, bits, q_ref, own_ref, left_ref, right_ref, f0, f1, f2, f3, out_ref, s_ref, m_ref, l_ref, acc_ref):
    sides = (left_ref, left_ref, own_ref, own_ref, right_ref, right_ref)

    def tile(kind, b, n, slot):
        if n == SPAN:
            column = kind * 2 + slot if heads == 2 else 4 + kind
            return jnp.concatenate([f[:, lanes(column)] for f in (f0, f1, f2, f3)], axis=0)
        return sides[b + n][:, lanes((kind * 2 + (b + n) % 2) * heads + slot)]

    for slot in range(heads):
        for b in range(2):
            here = lanes(b * heads + slot)
            query = q_ref[:, here]
            m_ref[...] = jnp.full_like(m_ref, -jnp.inf)
            l_ref[...] = jnp.zeros_like(l_ref)
            acc_ref[...] = jnp.zeros_like(acc_ref)
            for n in range(SPAN + 1):

                @pl.when(bits[b, n] > 0)
                def _():
                    s = lax.dot_general(
                        query, tile(0, b, n, slot), (((1,), (1,)), ((), ())), preferred_element_type=F32
                    )
                    s_ref[n] = s
                    m = m_ref[...]
                    for c in range(BLOCK // HEAD_DIM):
                        m = jnp.maximum(m, s[:, lanes(c)])
                    m_ref[...] = m

            m_ref[...] = jnp.broadcast_to(jnp.max(m_ref[...], axis=1, keepdims=True), m_ref.shape)
            for n in range(SPAN + 1):

                @pl.when(bits[b, n] > 0)
                def _():
                    peak = m_ref[...]
                    total = l_ref[...]
                    parts = []
                    for c in range(BLOCK // HEAD_DIM):
                        w = jnp.exp2((s_ref[n, :, lanes(c)] - peak) * RATE)
                        total = total + w
                        parts.append(w.astype(BF))
                    l_ref[...] = total
                    acc_ref[...] += jnp.dot(
                        jnp.concatenate(parts, axis=1), tile(1, b, n, slot), preferred_element_type=F32
                    )

            total = jnp.sum(l_ref[...], axis=1, keepdims=True)
            out_ref[:, here] = (acc_ref[...] / total).astype(BF)


def attention(heads, bits, query, own, left, right, first):
    pairs = heads * 2 * (SPAN + 1)
    return pl.pallas_call(
        lambda *refs: attention_kernel(heads, *refs),
        out_shape=jax.ShapeDtypeStruct(query.shape, BF),
        in_specs=[SMEM] + [VMEM] * 8,
        out_specs=VMEM,
        scratch_shapes=[
            pltpu.VMEM((SPAN + 1, BLOCK, BLOCK), F32),
            pltpu.VMEM((BLOCK, HEAD_DIM), F32),
            pltpu.VMEM((BLOCK, HEAD_DIM), F32),
            pltpu.VMEM((BLOCK, HEAD_DIM), F32),
        ],
        compiler_params=pltpu.CompilerParams(vmem_limit_bytes=32 << 20),
        cost_estimate=pl.CostEstimate(
            flops=pairs * 4 * BLOCK * BLOCK * HEAD_DIM,
            bytes_accessed=heads * 16 * BLOCK * HEAD_DIM * 2,
            transcendentals=pairs * BLOCK * BLOCK,
        ),
    )(bits, query, own, left, right, *first)


def mix_kernel(moves, moved_ref, q1_ref, k1_ref, v1_ref, query_ref, own_ref):
    kept = (q1_ref, k1_ref, v1_ref)

    def target(n):
        return (query_ref, lanes(n)) if n < 4 else (own_ref, lanes(n - 4))

    for n in range(12):
        out_ref, here = target(n)
        if n % 2 == 0:
            out_ref[:, here] = moved_ref[:, lanes(n)]

    @pl.when(moves[0] > 0)
    def _():
        for n in range(1, 12, 2):
            out_ref, here = target(n)
            out_ref[:, here] = moved_ref[:, lanes(n)]

    @pl.when(moves[0] <= 0)
    def _():
        for n in range(1, 12, 2):
            out_ref, here = target(n)
            b = n // 2 % 2
            out_ref[:, here] = kept[n // 4][b * BLOCK : (b + 1) * BLOCK, :]


def mix(moves, moved, kept):
    return pl.pallas_call(
        mix_kernel,
        out_shape=(
            jax.ShapeDtypeStruct((BLOCK, 4 * HEAD_DIM), BF),
            jax.ShapeDtypeStruct((BLOCK, 8 * HEAD_DIM), BF),
        ),
        in_specs=[SMEM] + [VMEM] * 4,
        out_specs=(VMEM, VMEM),
        compiler_params=pltpu.CompilerParams(vmem_limit_bytes=16 << 20),
    )(moves, moved, *kept)


def unpack_kernel(moves, x_ref, quarter_ref, w_ref):
    deep = x_ref.shape[0]
    blocks = w_ref.shape[1] // HEAD_DIM
    rows = w_ref.shape[0] // deep
    base = blocks * rows
    near = BLOCK // 4 // deep
    share = BLOCK // 16
    for z in range(deep):
        for c in range(blocks):
            w_ref[z * rows : (z + 1) * rows, lanes(c)] = x_ref[z, c * rows : (c + 1) * rows, :]
    pairs = [x_ref[z, base : base + 4 * near, :].astype(F32) for z in range(deep)]
    moving = [
        jnp.concatenate([pair[n * near : (n + 1) * near] for pair in pairs], axis=0).astype(BF) for n in range(4)
    ]
    base += 4 * near
    still = [
        jnp.concatenate(
            [x_ref[z, base + n * share : base + (n + 1) * share, :] for z in range(0, deep, deep // 4)], axis=0
        )
        for n in range(4)
    ]
    flag = moves[0] > 0
    quarter_ref[:, lanes(0)] = moving[0]
    quarter_ref[:, lanes(2)] = moving[2]
    quarter_ref[:, lanes(4)] = still[1]
    quarter_ref[:, lanes(5)] = still[3]
    quarter_ref[:, lanes(1)] = jnp.where(flag, moving[1].astype(F32), still[0].astype(F32)).astype(BF)
    quarter_ref[:, lanes(3)] = jnp.where(flag, moving[3].astype(F32), still[2].astype(F32)).astype(BF)


def unpack(moves, x, w_rows, w_cols):
    return pl.pallas_call(
        unpack_kernel,
        out_shape=(
            jax.ShapeDtypeStruct((BLOCK // 4, 6 * HEAD_DIM), BF),
            jax.ShapeDtypeStruct((w_rows, w_cols), BF),
        ),
        in_specs=[SMEM, VMEM],
        out_specs=(VMEM, VMEM),
        compiler_params=pltpu.CompilerParams(vmem_limit_bytes=16 << 20),
        cost_estimate=pl.CostEstimate(flops=COVER, bytes_accessed=0, transcendentals=0),
    )(moves, x)


def spatial_kernel(groups, order, spatial_ref, w_ref, part_ref, mixed_w_ref):
    def rows(g, slot):
        return w_ref[pl.ds(pl.multiple_of(order[g * 3 + slot] * HEAD_DIM, HEAD_DIM), HEAD_DIM), :]

    for g in range(groups):
        for slot in range(2):
            mixed_w_ref[(2 * g + slot) * HEAD_DIM : (2 * g + slot + 1) * HEAD_DIM, :] = rows(g, slot)
    chosen = jnp.concatenate([rows(g, 2) for g in range(groups)], axis=0)
    part_ref[...] = jnp.dot(spatial_ref[...], chosen, preferred_element_type=F32)


def spatial_projection(groups, order, spatial, w):
    return pl.pallas_call(
        lambda *refs: spatial_kernel(groups, *refs),
        out_shape=(
            jax.ShapeDtypeStruct((spatial.shape[0], w.shape[1]), F32),
            jax.ShapeDtypeStruct((groups * 2 * HEAD_DIM, w.shape[1]), BF),
        ),
        in_specs=[SMEM] + [VMEM] * 2,
        out_specs=(VMEM, VMEM),
        compiler_params=pltpu.CompilerParams(vmem_limit_bytes=32 << 20),
    )(order, spatial, w)


def mixed_kernel(part_ref, mixed_ref, w_ref, out_ref):
    out_ref[...] = (part_ref[...] + jnp.dot(mixed_ref[...], w_ref[...], preferred_element_type=F32)).astype(BF)


def mixed_projection(part, mixed, w):
    rows, cols = part.shape
    tile = rows // 4
    return pl.pallas_call(
        mixed_kernel,
        out_shape=jax.ShapeDtypeStruct((rows, cols), BF),
        grid=(rows // tile,),
        in_specs=[
            pl.BlockSpec((tile, cols), lambda i: (i, 0)),
            pl.BlockSpec((tile, mixed.shape[1]), lambda i: (i, 0)),
            pl.BlockSpec(w.shape, lambda i: (0, 0)),
        ],
        out_specs=pl.BlockSpec((tile, cols), lambda i: (i, 0)),
        compiler_params=pltpu.CompilerParams(vmem_limit_bytes=32 << 20),
    )(part, mixed, w)


def slots_of(labels):
    temporal = labels == 1
    a = jnp.where(temporal[:, 0], 0, jnp.where(temporal[:, 1], 1, 2))
    c = jnp.where(~temporal[:, 2], 2, jnp.where(~temporal[:, 1], 1, 0))
    return jnp.stack([a, 3 - a - c, c], axis=1).astype(jnp.int32)


def split_blocks(x):
    return jnp.concatenate([x[:BLOCK], x[BLOCK:]], axis=1)


def position_pack(x, parts):
    rows = x.shape[0] // parts // 2
    return x.reshape(parts, 2, rows, x.shape[1]).transpose(0, 2, 1, 3).reshape(parts, rows, 2 * x.shape[1])


def exchange(x):
    return lax.all_to_all(x, "ctx", 0, 0, tiled=True)


def both_ways(x, count):
    left = lax.ppermute(x, "ctx", [(i, i + 1) for i in range(count - 1)])
    right = lax.ppermute(x, "ctx", [(i + 1, i) for i in range(count - 1)])
    return left, right


def scattered(x, index, unit, live):
    count = lax.axis_size("ctx")
    rows = x.shape[0] // 4
    out = x[:rows]
    for k in (1, 2, 3):
        got = lax.ppermute(x[k * rows : (k + 1) * rows], "ctx", [(i, i + k * unit) for i in range(0, count, live)])
        out = jnp.where(index == k, got, out)
    return out


def body(queries, keys, values, block_mask, head_labels, w_out):
    parts = lax.axis_size("ctx")
    groups = lax.axis_size("head")
    place = lax.axis_index("ctx")
    group = lax.axis_index("head")
    deep = parts // 4
    y_lines = [[y * deep + z for y in range(4)] for z in range(deep)]
    along_z = [[y * deep + z for z in range(deep)] for y in range(4)]
    slots = slots_of(head_labels.reshape(groups, 3))
    mine = lax.dynamic_slice_in_dim(slots, group, 1, 0)[0]
    labels = lax.dynamic_slice_in_dim(head_labels, group * 3, 3)
    moves = lax.dynamic_slice_in_dim(labels, mine[1], 1)
    order = (slots + 3 * jnp.arange(groups, dtype=jnp.int32)[:, None]).reshape(-1)

    def head_of(x, slot):
        return lax.dynamic_slice_in_dim(x, mine[slot] * HEAD_DIM, HEAD_DIM, 1)

    q0, q1, q2 = (head_of(queries, s) for s in range(3))
    k0, k1, k2 = (head_of(keys, s) for s in range(3))
    v0, v1, v2 = (head_of(values, s) for s in range(3))

    index = place * 2 + jnp.arange(2, dtype=jnp.int32)
    total_blocks = block_mask.shape[0]
    rows = lax.dynamic_slice_in_dim(block_mask, place * 2, 2, 0)
    cand = index[:, None] + jnp.arange(-REACH, REACH + 1, dtype=jnp.int32)[None, :]
    every = jnp.arange(total_blocks, dtype=jnp.int32)
    hits = jnp.any((cand[:, :, None] == every[None, None, :]) & (rows[:, None, :] == 1), axis=2)
    first_bit = (index > REACH) & (rows[:, 0] == 1)
    bits = jnp.concatenate([hits, first_bit[:, None]], axis=1).astype(jnp.int32)

    shares = jnp.concatenate([k1, k2, v1, v2], axis=1)[:BLOCK]
    shares = scattered(shares, place // deep, deep, parts)
    shares = scattered(shares, place % deep // (deep // 4), deep // 4, deep)

    packs = [position_pack(jnp.concatenate(pair, axis=1), parts) for pair in ((q0, q1), (k0, k1), (v0, v1))]
    near = BLOCK // parts
    sent = jnp.concatenate(
        [w_out[:, lanes(c)] for c in range(w_out.shape[1] // HEAD_DIM)]
        + [x[:near] for x in (k0, k1, v0, v1)]
        + [shares[:, lanes(c)] for c in range(4)],
        axis=0,
    )
    own2 = jnp.concatenate([split_blocks(k2), split_blocks(v2)], axis=1)
    packed, sent = lax.optimization_barrier((jnp.concatenate(packs, axis=2), sent))
    moved = exchange(packed).reshape(BLOCK, -1)
    rows_z = lax.all_gather(sent, "ctx", axis=0, axis_index_groups=along_z)
    quarter, w_z = unpack(moves, rows_z, deep * w_out.shape[0], w_out.shape[1])
    moved, quarter = lax.optimization_barrier((moved, quarter))
    query, own = mix(moves, moved, (q1, k1, v1))
    left, right = both_ways(own, parts)

    def along_y(x):
        return [lax.ppermute(x, "ctx", [(i, i ^ (deep * k)) for i in range(parts)]) for k in (1, 2, 3)]

    first = [quarter] + along_y(quarter)
    left, right, first = lax.optimization_barrier((left, right, first))
    w_z, *first = lax.optimization_barrier((w_z, *first))
    w = lax.all_gather(w_z, "ctx", axis=0, axis_index_groups=y_lines, tiled=True)

    out = attention(2, bits, query, own, left, right, first)
    own2, _, _ = lax.optimization_barrier((own2, left, right))
    query2, _ = lax.optimization_barrier((split_blocks(q2), out))
    out2 = attention(1, bits, query2, own2, *both_ways(own2, parts), first)
    attn2 = jnp.concatenate([out2[:, lanes(0)], out2[:, lanes(1)]], axis=0)
    spatial = lax.all_gather(attn2, "head", axis=1, tiled=True)

    back = exchange(out.reshape(parts, BLOCK // parts, -1))
    back = back.reshape(parts, BLOCK // parts, 2, 2 * HEAD_DIM).transpose(0, 2, 1, 3).reshape(2 * BLOCK, 2 * HEAD_DIM)
    still = jnp.concatenate([out[:, lanes(1)], out[:, lanes(3)]], axis=0)
    attn = jnp.concatenate([back[:, lanes(0)], jnp.where(moves[0] > 0, back[:, lanes(1)], still)], axis=1)
    mixed = lax.all_gather(attn, "head", axis=1, tiled=True)
    part, mixed_w = spatial_projection(groups, order, spatial, w)
    return mixed_projection(part, mixed, mixed_w)


def solution(mesh):
    return jax.shard_map(
        body,
        mesh=mesh,
        in_specs=(P("ctx", "head"), P("ctx", "head"), P("ctx", "head"), P(), P(), P("ctx", "head")),
        out_specs=P("ctx", "head"),
        check_vma=False,
    )
```

```python
import math

import jax
import jax.numpy as jnp
from jax import lax
from jax.experimental import pallas as pl
from jax.experimental.pallas import tpu as pltpu
from jax.sharding import PartitionSpec as P

HEAD_DIM = 128
BLOCK = 512
REACH = 2
BF = jnp.bfloat16
F32 = jnp.float32
RATE = math.log2(math.e) / math.sqrt(HEAD_DIM)
SPAN = 2 * REACH + 1
COVER = 1 << 36


def lanes(index):
    return slice(index * HEAD_DIM, (index + 1) * HEAD_DIM)


VMEM = pl.BlockSpec(memory_space=pltpu.VMEM)
SMEM = pl.BlockSpec(memory_space=pltpu.SMEM)


def attention_kernel(heads, bits, q_ref, own_ref, left_ref, right_ref, f0, f1, f2, f3, out_ref, s_ref, m_ref, l_ref, acc_ref):
    sides = (left_ref, left_ref, own_ref, own_ref, right_ref, right_ref)

    def tile(kind, b, n, slot):
        if n == SPAN:
            column = kind * 2 + slot if heads == 2 else 4 + kind
            return jnp.concatenate([f[:, lanes(column)] for f in (f0, f1, f2, f3)], axis=0)
        return sides[b + n][:, lanes((kind * 2 + (b + n) % 2) * heads + slot)]

    for slot in range(heads):
        for b in range(2):
            here = lanes(b * heads + slot)
            query = q_ref[:, here]
            m_ref[...] = jnp.full_like(m_ref, -jnp.inf)
            l_ref[...] = jnp.zeros_like(l_ref)
            acc_ref[...] = jnp.zeros_like(acc_ref)
            for n in range(SPAN + 1):

                @pl.when(bits[b, n] > 0)
                def _():
                    s = lax.dot_general(
                        query, tile(0, b, n, slot), (((1,), (1,)), ((), ())), preferred_element_type=F32
                    )
                    s_ref[n] = s
                    m = m_ref[...]
                    for c in range(BLOCK // HEAD_DIM):
                        m = jnp.maximum(m, s[:, lanes(c)])
                    m_ref[...] = m

            m_ref[...] = jnp.broadcast_to(jnp.max(m_ref[...], axis=1, keepdims=True), m_ref.shape)
            for n in range(SPAN + 1):

                @pl.when(bits[b, n] > 0)
                def _():
                    peak = m_ref[...]
                    total = l_ref[...]
                    parts = []
                    for c in range(BLOCK // HEAD_DIM):
                        w = jnp.exp2((s_ref[n, :, lanes(c)] - peak) * RATE)
                        total = total + w
                        parts.append(w.astype(BF))
                    l_ref[...] = total
                    acc_ref[...] += jnp.dot(
                        jnp.concatenate(parts, axis=1), tile(1, b, n, slot), preferred_element_type=F32
                    )

            total = jnp.sum(l_ref[...], axis=1, keepdims=True)
            out_ref[:, here] = (acc_ref[...] / total).astype(BF)


def attention(heads, bits, query, own, left, right, first):
    pairs = heads * 2 * (SPAN + 1)
    return pl.pallas_call(
        lambda *refs: attention_kernel(heads, *refs),
        out_shape=jax.ShapeDtypeStruct(query.shape, BF),
        in_specs=[SMEM] + [VMEM] * 8,
        out_specs=VMEM,
        scratch_shapes=[
            pltpu.VMEM((SPAN + 1, BLOCK, BLOCK), F32),
            pltpu.VMEM((BLOCK, HEAD_DIM), F32),
            pltpu.VMEM((BLOCK, HEAD_DIM), F32),
            pltpu.VMEM((BLOCK, HEAD_DIM), F32),
        ],
        compiler_params=pltpu.CompilerParams(vmem_limit_bytes=32 << 20),
        cost_estimate=pl.CostEstimate(
            flops=pairs * 4 * BLOCK * BLOCK * HEAD_DIM,
            bytes_accessed=heads * 16 * BLOCK * HEAD_DIM * 2,
            transcendentals=pairs * BLOCK * BLOCK,
        ),
    )(bits, query, own, left, right, *first)


def mix_kernel(moves, moved_ref, q1_ref, k1_ref, v1_ref, query_ref, own_ref):
    kept = (q1_ref, k1_ref, v1_ref)

    def target(n):
        return (query_ref, lanes(n)) if n < 4 else (own_ref, lanes(n - 4))

    for n in range(12):
        out_ref, here = target(n)
        if n % 2 == 0:
            out_ref[:, here] = moved_ref[:, lanes(n)]

    @pl.when(moves[0] > 0)
    def _():
        for n in range(1, 12, 2):
            out_ref, here = target(n)
            out_ref[:, here] = moved_ref[:, lanes(n)]

    @pl.when(moves[0] <= 0)
    def _():
        for n in range(1, 12, 2):
            out_ref, here = target(n)
            b = n // 2 % 2
            out_ref[:, here] = kept[n // 4][b * BLOCK : (b + 1) * BLOCK, :]


def mix(moves, moved, kept):
    return pl.pallas_call(
        mix_kernel,
        out_shape=(
            jax.ShapeDtypeStruct((BLOCK, 4 * HEAD_DIM), BF),
            jax.ShapeDtypeStruct((BLOCK, 8 * HEAD_DIM), BF),
        ),
        in_specs=[SMEM] + [VMEM] * 4,
        out_specs=(VMEM, VMEM),
        compiler_params=pltpu.CompilerParams(vmem_limit_bytes=16 << 20),
    )(moves, moved, *kept)


def unpack_kernel(moves, x_ref, quarter_ref, w_ref):
    deep = x_ref.shape[0]
    blocks = w_ref.shape[1] // HEAD_DIM
    rows = w_ref.shape[0] // deep
    base = blocks * rows
    near = BLOCK // 4 // deep
    share = BLOCK // 16
    for z in range(deep):
        for c in range(blocks):
            w_ref[z * rows : (z + 1) * rows, lanes(c)] = x_ref[z, c * rows : (c + 1) * rows, :]
    pairs = [x_ref[z, base : base + 4 * near, :].astype(F32) for z in range(deep)]
    moving = [
        jnp.concatenate([pair[n * near : (n + 1) * near] for pair in pairs], axis=0).astype(BF) for n in range(4)
    ]
    base += 4 * near
    still = [
        jnp.concatenate(
            [x_ref[z, base + n * share : base + (n + 1) * share, :] for z in range(0, deep, deep // 4)], axis=0
        )
        for n in range(4)
    ]
    flag = moves[0] > 0
    quarter_ref[:, lanes(0)] = moving[0]
    quarter_ref[:, lanes(2)] = moving[2]
    quarter_ref[:, lanes(4)] = still[1]
    quarter_ref[:, lanes(5)] = still[3]
    quarter_ref[:, lanes(1)] = jnp.where(flag, moving[1].astype(F32), still[0].astype(F32)).astype(BF)
    quarter_ref[:, lanes(3)] = jnp.where(flag, moving[3].astype(F32), still[2].astype(F32)).astype(BF)


def unpack(moves, x, w_rows, w_cols):
    return pl.pallas_call(
        unpack_kernel,
        out_shape=(
            jax.ShapeDtypeStruct((BLOCK // 4, 6 * HEAD_DIM), BF),
            jax.ShapeDtypeStruct((w_rows, w_cols), BF),
        ),
        in_specs=[SMEM, VMEM],
        out_specs=(VMEM, VMEM),
        compiler_params=pltpu.CompilerParams(vmem_limit_bytes=16 << 20),
        cost_estimate=pl.CostEstimate(flops=COVER, bytes_accessed=0, transcendentals=0),
    )(moves, x)


def order_kernel(order, w_ref, out_ref):
    for n in range(w_ref.shape[0] // HEAD_DIM):
        out_ref[n * HEAD_DIM : (n + 1) * HEAD_DIM, :] = w_ref[
            pl.ds(pl.multiple_of(order[n] * HEAD_DIM, HEAD_DIM), HEAD_DIM), :
        ]


def slot_order(order, w):
    return pl.pallas_call(
        order_kernel,
        out_shape=jax.ShapeDtypeStruct(w.shape, BF),
        in_specs=[SMEM, VMEM],
        out_specs=VMEM,
        compiler_params=pltpu.CompilerParams(vmem_limit_bytes=16 << 20),
    )(order, w)


def projection_kernel(attn_ref, w_ref, out_ref):
    out_ref[...] = jnp.dot(attn_ref[...], w_ref[...], preferred_element_type=F32).astype(BF)


def projection(attn, w):
    rows, depth = attn.shape
    cols = w.shape[1]
    tile = rows // 8
    return pl.pallas_call(
        projection_kernel,
        out_shape=jax.ShapeDtypeStruct((rows, cols), BF),
        grid=(rows // tile,),
        in_specs=[pl.BlockSpec((tile, depth), lambda i: (i, 0)), pl.BlockSpec((depth, cols), lambda i: (0, 0))],
        out_specs=pl.BlockSpec((tile, cols), lambda i: (i, 0)),
        compiler_params=pltpu.CompilerParams(vmem_limit_bytes=56 << 20),
    )(attn, w)


def slots_of(labels):
    temporal = labels == 1
    a = jnp.where(temporal[:, 0], 0, jnp.where(temporal[:, 1], 1, 2))
    c = jnp.where(~temporal[:, 2], 2, jnp.where(~temporal[:, 1], 1, 0))
    return jnp.stack([a, 3 - a - c, c], axis=1).astype(jnp.int32)


def split_blocks(x):
    return jnp.concatenate([x[:BLOCK], x[BLOCK:]], axis=1)


def position_pack(x, parts):
    rows = x.shape[0] // parts // 2
    return x.reshape(parts, 2, rows, x.shape[1]).transpose(0, 2, 1, 3).reshape(parts, rows, 2 * x.shape[1])


def exchange(x):
    return lax.all_to_all(x, "ctx", 0, 0, tiled=True)


def both_ways(x, count):
    left = lax.ppermute(x, "ctx", [(i, i + 1) for i in range(count - 1)])
    right = lax.ppermute(x, "ctx", [(i + 1, i) for i in range(count - 1)])
    return left, right


def scattered(x, index, unit, live):
    count = lax.axis_size("ctx")
    rows = x.shape[0] // 4
    out = x[:rows]
    for k in (1, 2, 3):
        got = lax.ppermute(x[k * rows : (k + 1) * rows], "ctx", [(i, i + k * unit) for i in range(0, count, live)])
        out = jnp.where(index == k, got, out)
    return out


def body(queries, keys, values, block_mask, head_labels, w_out):
    parts = lax.axis_size("ctx")
    groups = lax.axis_size("head")
    place = lax.axis_index("ctx")
    group = lax.axis_index("head")
    deep = parts // 4
    y_lines = [[y * deep + z for y in range(4)] for z in range(deep)]
    along_z = [[y * deep + z for z in range(deep)] for y in range(4)]
    slots = slots_of(head_labels.reshape(groups, 3))
    mine = lax.dynamic_slice_in_dim(slots, group, 1, 0)[0]
    labels = lax.dynamic_slice_in_dim(head_labels, group * 3, 3)
    moves = lax.dynamic_slice_in_dim(labels, mine[1], 1)
    order = (slots + 3 * jnp.arange(groups, dtype=jnp.int32)[:, None]).reshape(-1)

    def head_of(x, slot):
        return lax.dynamic_slice_in_dim(x, mine[slot] * HEAD_DIM, HEAD_DIM, 1)

    q0, q1, q2 = (head_of(queries, s) for s in range(3))
    k0, k1, k2 = (head_of(keys, s) for s in range(3))
    v0, v1, v2 = (head_of(values, s) for s in range(3))

    index = place * 2 + jnp.arange(2, dtype=jnp.int32)
    total_blocks = block_mask.shape[0]
    rows = lax.dynamic_slice_in_dim(block_mask, place * 2, 2, 0)
    cand = index[:, None] + jnp.arange(-REACH, REACH + 1, dtype=jnp.int32)[None, :]
    every = jnp.arange(total_blocks, dtype=jnp.int32)
    hits = jnp.any((cand[:, :, None] == every[None, None, :]) & (rows[:, None, :] == 1), axis=2)
    first_bit = (index > REACH) & (rows[:, 0] == 1)
    bits = jnp.concatenate([hits, first_bit[:, None]], axis=1).astype(jnp.int32)

    shares = jnp.concatenate([k1, k2, v1, v2], axis=1)[:BLOCK]
    shares = scattered(shares, place // deep, deep, parts)
    shares = scattered(shares, place % deep // (deep // 4), deep // 4, deep)

    packs = [position_pack(jnp.concatenate(pair, axis=1), parts) for pair in ((q0, q1), (k0, k1), (v0, v1))]
    near = BLOCK // parts
    sent = jnp.concatenate(
        [w_out[:, lanes(c)] for c in range(w_out.shape[1] // HEAD_DIM)]
        + [x[:near] for x in (k0, k1, v0, v1)]
        + [shares[:, lanes(c)] for c in range(4)],
        axis=0,
    )
    own2 = jnp.concatenate([split_blocks(k2), split_blocks(v2)], axis=1)
    packed, sent = lax.optimization_barrier((jnp.concatenate(packs, axis=2), sent))
    moved = exchange(packed).reshape(BLOCK, -1)
    rows_z = lax.all_gather(sent, "ctx", axis=0, axis_index_groups=along_z)
    rows_z, own2, query2, bits = lax.optimization_barrier((rows_z, own2, split_blocks(q2), bits))
    quarter, w_z = unpack(moves, rows_z, deep * w_out.shape[0], w_out.shape[1])
    moved, quarter = lax.optimization_barrier((moved, quarter))
    query, own = mix(moves, moved, (q1, k1, v1))
    left, right = both_ways(own, parts)

    def along_y(x):
        return [lax.ppermute(x, "ctx", [(i, i ^ (deep * k)) for i in range(parts)]) for k in (1, 2, 3)]

    first = [quarter] + along_y(quarter)
    left, right, first = lax.optimization_barrier((left, right, first))
    w_z, *first = lax.optimization_barrier((w_z, *first))
    w = lax.all_gather(w_z, "ctx", axis=0, axis_index_groups=y_lines, tiled=True)

    out = attention(2, bits, query, own, left, right, first)
    own2, _, _ = lax.optimization_barrier((own2, left, right))
    out, left2, right2 = lax.optimization_barrier((out, *both_ways(own2, parts)))
    out2 = attention(1, bits, query2, own2, left2, right2, first)
    attn2 = jnp.concatenate([out2[:, lanes(0)], out2[:, lanes(1)]], axis=0)

    back = exchange(out.reshape(parts, BLOCK // parts, -1))
    back = back.reshape(parts, BLOCK // parts, 2, 2 * HEAD_DIM).transpose(0, 2, 1, 3).reshape(2 * BLOCK, 2 * HEAD_DIM)
    still = jnp.concatenate([out[:, lanes(1)], out[:, lanes(3)]], axis=0)
    attn = jnp.concatenate([back[:, lanes(0)], jnp.where(moves[0] > 0, back[:, lanes(1)], still), attn2], axis=1)
    return projection(lax.all_gather(attn, "head", axis=1, tiled=True), slot_order(order, w))


def solution(mesh):
    return jax.shard_map(
        body,
        mesh=mesh,
        in_specs=(P("ctx", "head"), P("ctx", "head"), P("ctx", "head"), P(), P(), P("ctx", "head")),
        out_specs=P("ctx", "head"),
        check_vma=False,
    )
```

```python
import math

import jax
import jax.numpy as jnp
from jax import lax
from jax.experimental import pallas as pl
from jax.experimental.pallas import tpu as pltpu
from jax.sharding import PartitionSpec as P

HEAD_DIM = 128
BLOCK = 512
REACH = 2
BF = jnp.bfloat16
F32 = jnp.float32
RATE = math.log2(math.e) / math.sqrt(HEAD_DIM)
SPAN = 2 * REACH + 1
COVER = 1 << 36


def lanes(index):
    return slice(index * HEAD_DIM, (index + 1) * HEAD_DIM)


VMEM = pl.BlockSpec(memory_space=pltpu.VMEM)
SMEM = pl.BlockSpec(memory_space=pltpu.SMEM)


def attention_kernel(heads, bits, q_ref, own_ref, left_ref, right_ref, f0, f1, f2, f3, out_ref, s_ref, m_ref, l_ref, acc_ref):
    sides = (left_ref, left_ref, own_ref, own_ref, right_ref, right_ref)

    def tile(kind, b, n, slot):
        if n == SPAN:
            column = kind * 2 + slot if heads == 2 else 4 + kind
            return jnp.concatenate([f[:, lanes(column)] for f in (f0, f1, f2, f3)], axis=0)
        return sides[b + n][:, lanes((kind * 2 + (b + n) % 2) * heads + slot)]

    for slot in range(heads):
        for b in range(2):
            here = lanes(b * heads + slot)
            query = q_ref[:, here]
            m_ref[...] = jnp.full_like(m_ref, -jnp.inf)
            l_ref[...] = jnp.zeros_like(l_ref)
            acc_ref[...] = jnp.zeros_like(acc_ref)
            for n in range(SPAN + 1):

                @pl.when(bits[b, n] > 0)
                def _():
                    s = lax.dot_general(
                        query, tile(0, b, n, slot), (((1,), (1,)), ((), ())), preferred_element_type=F32
                    )
                    s_ref[n] = s
                    m = m_ref[...]
                    for c in range(BLOCK // HEAD_DIM):
                        m = jnp.maximum(m, s[:, lanes(c)])
                    m_ref[...] = m

            m_ref[...] = jnp.broadcast_to(jnp.max(m_ref[...], axis=1, keepdims=True), m_ref.shape)
            for n in range(SPAN + 1):

                @pl.when(bits[b, n] > 0)
                def _():
                    peak = m_ref[...]
                    total = l_ref[...]
                    parts = []
                    for c in range(BLOCK // HEAD_DIM):
                        w = jnp.exp2((s_ref[n, :, lanes(c)] - peak) * RATE)
                        total = total + w
                        parts.append(w.astype(BF))
                    l_ref[...] = total
                    acc_ref[...] += jnp.dot(
                        jnp.concatenate(parts, axis=1), tile(1, b, n, slot), preferred_element_type=F32
                    )

            total = jnp.sum(l_ref[...], axis=1, keepdims=True)
            out_ref[:, here] = (acc_ref[...] / total).astype(BF)


def attention(heads, bits, query, own, left, right, first):
    pairs = heads * 2 * (SPAN + 1)
    return pl.pallas_call(
        lambda *refs: attention_kernel(heads, *refs),
        out_shape=jax.ShapeDtypeStruct(query.shape, BF),
        in_specs=[SMEM] + [VMEM] * 8,
        out_specs=VMEM,
        scratch_shapes=[
            pltpu.VMEM((SPAN + 1, BLOCK, BLOCK), F32),
            pltpu.VMEM((BLOCK, HEAD_DIM), F32),
            pltpu.VMEM((BLOCK, HEAD_DIM), F32),
            pltpu.VMEM((BLOCK, HEAD_DIM), F32),
        ],
        compiler_params=pltpu.CompilerParams(vmem_limit_bytes=32 << 20),
        cost_estimate=pl.CostEstimate(
            flops=pairs * 4 * BLOCK * BLOCK * HEAD_DIM,
            bytes_accessed=heads * 16 * BLOCK * HEAD_DIM * 2,
            transcendentals=pairs * BLOCK * BLOCK,
        ),
    )(bits, query, own, left, right, *first)


def mix_kernel(moves, moved_ref, q1_ref, k1_ref, v1_ref, query_ref, own_ref):
    kept = (q1_ref, k1_ref, v1_ref)

    def target(n):
        return (query_ref, lanes(n)) if n < 4 else (own_ref, lanes(n - 4))

    for n in range(12):
        out_ref, here = target(n)
        if n % 2 == 0:
            out_ref[:, here] = moved_ref[:, lanes(n)]

    @pl.when(moves[0] > 0)
    def _():
        for n in range(1, 12, 2):
            out_ref, here = target(n)
            out_ref[:, here] = moved_ref[:, lanes(n)]

    @pl.when(moves[0] <= 0)
    def _():
        for n in range(1, 12, 2):
            out_ref, here = target(n)
            b = n // 2 % 2
            out_ref[:, here] = kept[n // 4][b * BLOCK : (b + 1) * BLOCK, :]


def mix(moves, moved, kept):
    return pl.pallas_call(
        mix_kernel,
        out_shape=(
            jax.ShapeDtypeStruct((BLOCK, 4 * HEAD_DIM), BF),
            jax.ShapeDtypeStruct((BLOCK, 8 * HEAD_DIM), BF),
        ),
        in_specs=[SMEM] + [VMEM] * 4,
        out_specs=(VMEM, VMEM),
        compiler_params=pltpu.CompilerParams(vmem_limit_bytes=16 << 20),
    )(moves, moved, *kept)


def unpack_kernel(moves, x_ref, quarter_ref, w_ref):
    deep = x_ref.shape[0]
    blocks = w_ref.shape[1] // HEAD_DIM
    rows = w_ref.shape[0] // deep
    base = blocks * rows
    near = BLOCK // 4 // deep
    share = BLOCK // 16
    for z in range(deep):
        for c in range(blocks):
            w_ref[z * rows : (z + 1) * rows, lanes(c)] = x_ref[z, c * rows : (c + 1) * rows, :]
    pairs = [x_ref[z, base : base + 4 * near, :].astype(F32) for z in range(deep)]
    moving = [
        jnp.concatenate([pair[n * near : (n + 1) * near] for pair in pairs], axis=0).astype(BF) for n in range(4)
    ]
    base += 4 * near
    still = [
        jnp.concatenate(
            [x_ref[z, base + n * share : base + (n + 1) * share, :] for z in range(0, deep, deep // 4)], axis=0
        )
        for n in range(4)
    ]
    flag = moves[0] > 0
    quarter_ref[:, lanes(0)] = moving[0]
    quarter_ref[:, lanes(2)] = moving[2]
    quarter_ref[:, lanes(4)] = still[1]
    quarter_ref[:, lanes(5)] = still[3]
    quarter_ref[:, lanes(1)] = jnp.where(flag, moving[1].astype(F32), still[0].astype(F32)).astype(BF)
    quarter_ref[:, lanes(3)] = jnp.where(flag, moving[3].astype(F32), still[2].astype(F32)).astype(BF)


def unpack(moves, x, w_rows, w_cols):
    return pl.pallas_call(
        unpack_kernel,
        out_shape=(
            jax.ShapeDtypeStruct((BLOCK // 4, 6 * HEAD_DIM), BF),
            jax.ShapeDtypeStruct((w_rows, w_cols), BF),
        ),
        in_specs=[SMEM, VMEM],
        out_specs=(VMEM, VMEM),
        compiler_params=pltpu.CompilerParams(vmem_limit_bytes=16 << 20),
        cost_estimate=pl.CostEstimate(flops=COVER, bytes_accessed=0, transcendentals=0),
    )(moves, x)


def order_kernel(order, w_ref, out_ref):
    for n in range(w_ref.shape[0] // HEAD_DIM):
        out_ref[n * HEAD_DIM : (n + 1) * HEAD_DIM, :] = w_ref[
            pl.ds(pl.multiple_of(order[n] * HEAD_DIM, HEAD_DIM), HEAD_DIM), :
        ]


def slot_order(order, w):
    return pl.pallas_call(
        order_kernel,
        out_shape=jax.ShapeDtypeStruct(w.shape, BF),
        in_specs=[SMEM, VMEM],
        out_specs=VMEM,
        compiler_params=pltpu.CompilerParams(vmem_limit_bytes=16 << 20),
    )(order, w)


def projection_kernel(attn_ref, w_ref, out_ref, total_ref):
    part = jnp.dot(attn_ref[...], w_ref[...], preferred_element_type=F32)
    step = pl.program_id(0)
    last = pl.num_programs(0) - 1

    @pl.when(step == 0)
    def _():
        total_ref[...] = part

    @pl.when((step > 0) & (step < last))
    def _():
        total_ref[...] += part

    @pl.when(step == last)
    def _():
        out_ref[...] = (total_ref[...] + part).astype(BF)


def projection(attn, w):
    rows, depth = attn.shape
    cols = w.shape[1]
    steps = 4
    return pl.pallas_call(
        projection_kernel,
        out_shape=jax.ShapeDtypeStruct((rows, cols), BF),
        grid=(steps,),
        in_specs=[
            pl.BlockSpec((rows, depth // steps), lambda i: (0, i)),
            pl.BlockSpec((depth // steps, cols), lambda i: (i, 0)),
        ],
        out_specs=pl.BlockSpec((rows, cols), lambda i: (0, 0)),
        scratch_shapes=[pltpu.VMEM((rows, cols), F32)],
        compiler_params=pltpu.CompilerParams(vmem_limit_bytes=56 << 20),
    )(attn, w)


def slots_of(labels):
    temporal = labels == 1
    a = jnp.where(temporal[:, 0], 0, jnp.where(temporal[:, 1], 1, 2))
    c = jnp.where(~temporal[:, 2], 2, jnp.where(~temporal[:, 1], 1, 0))
    return jnp.stack([a, 3 - a - c, c], axis=1).astype(jnp.int32)


def split_blocks(x):
    return jnp.concatenate([x[:BLOCK], x[BLOCK:]], axis=1)


def position_pack(x, parts):
    rows = x.shape[0] // parts // 2
    return x.reshape(parts, 2, rows, x.shape[1]).transpose(0, 2, 1, 3).reshape(parts, rows, 2 * x.shape[1])


def exchange(x):
    return lax.all_to_all(x, "ctx", 0, 0, tiled=True)


def both_ways(x, count):
    left = lax.ppermute(x, "ctx", [(i, i + 1) for i in range(count - 1)])
    right = lax.ppermute(x, "ctx", [(i + 1, i) for i in range(count - 1)])
    return left, right


def scattered(x, index, unit, live):
    count = lax.axis_size("ctx")
    rows = x.shape[0] // 4
    out = x[:rows]
    for k in (1, 2, 3):
        got = lax.ppermute(x[k * rows : (k + 1) * rows], "ctx", [(i, i + k * unit) for i in range(0, count, live)])
        out = jnp.where(index == k, got, out)
    return out


def body(queries, keys, values, block_mask, head_labels, w_out):
    parts = lax.axis_size("ctx")
    groups = lax.axis_size("head")
    place = lax.axis_index("ctx")
    group = lax.axis_index("head")
    deep = parts // 4
    y_lines = [[y * deep + z for y in range(4)] for z in range(deep)]
    along_z = [[y * deep + z for z in range(deep)] for y in range(4)]
    slots = slots_of(head_labels.reshape(groups, 3))
    mine = lax.dynamic_slice_in_dim(slots, group, 1, 0)[0]
    labels = lax.dynamic_slice_in_dim(head_labels, group * 3, 3)
    moves = lax.dynamic_slice_in_dim(labels, mine[1], 1)
    order = (slots + 3 * jnp.arange(groups, dtype=jnp.int32)[:, None]).reshape(-1)

    def head_of(x, slot):
        return lax.dynamic_slice_in_dim(x, mine[slot] * HEAD_DIM, HEAD_DIM, 1)

    q0, q1, q2 = (head_of(queries, s) for s in range(3))
    k0, k1, k2 = (head_of(keys, s) for s in range(3))
    v0, v1, v2 = (head_of(values, s) for s in range(3))

    index = place * 2 + jnp.arange(2, dtype=jnp.int32)
    total_blocks = block_mask.shape[0]
    rows = lax.dynamic_slice_in_dim(block_mask, place * 2, 2, 0)
    cand = index[:, None] + jnp.arange(-REACH, REACH + 1, dtype=jnp.int32)[None, :]
    every = jnp.arange(total_blocks, dtype=jnp.int32)
    hits = jnp.any((cand[:, :, None] == every[None, None, :]) & (rows[:, None, :] == 1), axis=2)
    first_bit = (index > REACH) & (rows[:, 0] == 1)
    bits = jnp.concatenate([hits, first_bit[:, None]], axis=1).astype(jnp.int32)

    shares = jnp.concatenate([k1, k2, v1, v2], axis=1)[:BLOCK]
    shares = scattered(shares, place // deep, deep, parts)
    shares = scattered(shares, place % deep // (deep // 4), deep // 4, deep)

    packs = [position_pack(jnp.concatenate(pair, axis=1), parts) for pair in ((q0, q1), (k0, k1), (v0, v1))]
    near = BLOCK // parts
    sent = jnp.concatenate(
        [w_out[:, lanes(c)] for c in range(w_out.shape[1] // HEAD_DIM)]
        + [x[:near] for x in (k0, k1, v0, v1)]
        + [shares[:, lanes(c)] for c in range(4)],
        axis=0,
    )
    packed, sent = lax.optimization_barrier((jnp.concatenate(packs, axis=2), sent))
    moved = exchange(packed).reshape(BLOCK, -1)
    rows_z = lax.all_gather(sent, "ctx", axis=0, axis_index_groups=along_z)
    quarter, w_z = unpack(moves, rows_z, deep * w_out.shape[0], w_out.shape[1])
    q2, k2, v2, quarter = lax.optimization_barrier((q2, k2, v2, quarter))
    own2 = jnp.concatenate([split_blocks(k2), split_blocks(v2)], axis=1)
    query2 = split_blocks(q2)
    moved, quarter, own2 = lax.optimization_barrier((moved, quarter, own2))
    query, own = mix(moves, moved, (q1, k1, v1))
    left, right = both_ways(own, parts)

    def along_y(x):
        return [lax.ppermute(x, "ctx", [(i, i ^ (deep * k)) for i in range(parts)]) for k in (1, 2, 3)]

    first = [quarter] + along_y(quarter)
    left, right, first = lax.optimization_barrier((left, right, first))
    w_z, *first = lax.optimization_barrier((w_z, *first))
    w = lax.all_gather(w_z, "ctx", axis=0, axis_index_groups=y_lines, tiled=True)

    out = attention(2, bits, query, own, left, right, first)
    own2, _, _ = lax.optimization_barrier((own2, left, right))
    out, left2, right2 = lax.optimization_barrier((out, *both_ways(own2, parts)))
    out2 = attention(1, bits, query2, own2, left2, right2, first)
    attn2 = jnp.concatenate([out2[:, lanes(0)], out2[:, lanes(1)]], axis=0)

    back = exchange(out.reshape(parts, BLOCK // parts, -1))
    back = back.reshape(parts, BLOCK // parts, 2, 2 * HEAD_DIM).transpose(0, 2, 1, 3).reshape(2 * BLOCK, 2 * HEAD_DIM)
    still = jnp.concatenate([out[:, lanes(1)], out[:, lanes(3)]], axis=0)
    attn = jnp.concatenate([back[:, lanes(0)], jnp.where(moves[0] > 0, back[:, lanes(1)], still), attn2], axis=1)
    return projection(lax.all_gather(attn, "head", axis=1, tiled=True), slot_order(order, w))


def solution(mesh):
    return jax.shard_map(
        body,
        mesh=mesh,
        in_specs=(P("ctx", "head"), P("ctx", "head"), P("ctx", "head"), P(), P(), P("ctx", "head")),
        out_specs=P("ctx", "head"),
        check_vma=False,
    )
```

```python
import math

import jax
import jax.numpy as jnp
from jax import lax
from jax.experimental import pallas as pl
from jax.experimental.pallas import tpu as pltpu
from jax.sharding import PartitionSpec as P

HEAD_DIM = 128
BLOCK = 512
REACH = 2
BF = jnp.bfloat16
F32 = jnp.float32
RATE = math.log2(math.e) / math.sqrt(HEAD_DIM)
SPAN = 2 * REACH + 1
COVER = 1 << 36


def lanes(index):
    return slice(index * HEAD_DIM, (index + 1) * HEAD_DIM)


VMEM = pl.BlockSpec(memory_space=pltpu.VMEM)
SMEM = pl.BlockSpec(memory_space=pltpu.SMEM)


def attention_kernel(heads, bits, q_ref, own_ref, left_ref, right_ref, f0, f1, f2, f3, out_ref, s_ref, m_ref, l_ref, acc_ref):
    sides = (left_ref, left_ref, own_ref, own_ref, right_ref, right_ref)

    def tile(kind, b, n, slot):
        if n == SPAN:
            column = kind * 2 + slot if heads == 2 else 4 + kind
            return jnp.concatenate([f[:, lanes(column)] for f in (f0, f1, f2, f3)], axis=0)
        return sides[b + n][:, lanes((kind * 2 + (b + n) % 2) * heads + slot)]

    for slot in range(heads):
        for b in range(2):
            here = lanes(b * heads + slot)
            query = q_ref[:, here]
            m_ref[...] = jnp.full_like(m_ref, -jnp.inf)
            l_ref[...] = jnp.zeros_like(l_ref)
            acc_ref[...] = jnp.zeros_like(acc_ref)
            for n in range(SPAN + 1):

                @pl.when(bits[b, n] > 0)
                def _():
                    s = lax.dot_general(
                        query, tile(0, b, n, slot), (((1,), (1,)), ((), ())), preferred_element_type=F32
                    )
                    s_ref[n] = s
                    m = m_ref[...]
                    for c in range(BLOCK // HEAD_DIM):
                        m = jnp.maximum(m, s[:, lanes(c)])
                    m_ref[...] = m

            m_ref[...] = jnp.broadcast_to(jnp.max(m_ref[...], axis=1, keepdims=True), m_ref.shape)
            for n in range(SPAN + 1):

                @pl.when(bits[b, n] > 0)
                def _():
                    peak = m_ref[...]
                    total = l_ref[...]
                    parts = []
                    for c in range(BLOCK // HEAD_DIM):
                        w = jnp.exp2((s_ref[n, :, lanes(c)] - peak) * RATE)
                        total = total + w
                        parts.append(w.astype(BF))
                    l_ref[...] = total
                    acc_ref[...] += jnp.dot(
                        jnp.concatenate(parts, axis=1), tile(1, b, n, slot), preferred_element_type=F32
                    )

            total = jnp.sum(l_ref[...], axis=1, keepdims=True)
            out_ref[:, here] = (acc_ref[...] / total).astype(BF)


def attention(heads, bits, query, own, left, right, first):
    pairs = heads * 2 * (SPAN + 1)
    return pl.pallas_call(
        lambda *refs: attention_kernel(heads, *refs),
        out_shape=jax.ShapeDtypeStruct(query.shape, BF),
        in_specs=[SMEM] + [VMEM] * 8,
        out_specs=VMEM,
        scratch_shapes=[
            pltpu.VMEM((SPAN + 1, BLOCK, BLOCK), F32),
            pltpu.VMEM((BLOCK, HEAD_DIM), F32),
            pltpu.VMEM((BLOCK, HEAD_DIM), F32),
            pltpu.VMEM((BLOCK, HEAD_DIM), F32),
        ],
        compiler_params=pltpu.CompilerParams(vmem_limit_bytes=32 << 20),
        cost_estimate=pl.CostEstimate(
            flops=pairs * 4 * BLOCK * BLOCK * HEAD_DIM,
            bytes_accessed=heads * 16 * BLOCK * HEAD_DIM * 2,
            transcendentals=pairs * BLOCK * BLOCK,
        ),
    )(bits, query, own, left, right, *first)


def mix_kernel(moves, moved_ref, q1_ref, k1_ref, v1_ref, query_ref, own_ref):
    kept = (q1_ref, k1_ref, v1_ref)

    def target(n):
        return (query_ref, lanes(n)) if n < 4 else (own_ref, lanes(n - 4))

    for n in range(12):
        out_ref, here = target(n)
        if n % 2 == 0:
            out_ref[:, here] = moved_ref[:, lanes(n)]

    @pl.when(moves[0] > 0)
    def _():
        for n in range(1, 12, 2):
            out_ref, here = target(n)
            out_ref[:, here] = moved_ref[:, lanes(n)]

    @pl.when(moves[0] <= 0)
    def _():
        for n in range(1, 12, 2):
            out_ref, here = target(n)
            b = n // 2 % 2
            out_ref[:, here] = kept[n // 4][b * BLOCK : (b + 1) * BLOCK, :]


def mix(moves, moved, kept):
    return pl.pallas_call(
        mix_kernel,
        out_shape=(
            jax.ShapeDtypeStruct((BLOCK, 4 * HEAD_DIM), BF),
            jax.ShapeDtypeStruct((BLOCK, 8 * HEAD_DIM), BF),
        ),
        in_specs=[SMEM] + [VMEM] * 4,
        out_specs=(VMEM, VMEM),
        compiler_params=pltpu.CompilerParams(vmem_limit_bytes=16 << 20),
    )(moves, moved, *kept)


def payload_kernel(w_ref, k0, k1, v0, v1, shares_ref, out_ref):
    rows = w_ref.shape[0]
    share = shares_ref.shape[0]
    at = 0
    for c in range(w_ref.shape[1] // HEAD_DIM):
        out_ref[at : at + rows, :] = w_ref[:, lanes(c)]
        at += rows
    for a, b in ((k0, k1), (v0, v1)):
        near = a.shape[0] // 2
        both = [x[...].astype(F32)[:near] for x in (a, b)]
        out_ref[at : at + 2 * near, :] = jnp.concatenate(both, axis=0).astype(BF)
        at += 2 * near
    for n in range(4):
        out_ref[at : at + share, :] = shares_ref[:, lanes(n)]
        at += share


def payload(near, w_out, heads, shares):
    rows = w_out.size // HEAD_DIM + 4 * near + shares.size // HEAD_DIM

    def top(shape):
        return pl.BlockSpec(shape, lambda i: (0, 0))

    return pl.pallas_call(
        payload_kernel,
        out_shape=jax.ShapeDtypeStruct((rows, HEAD_DIM), BF),
        grid=(1,),
        in_specs=[top(w_out.shape)] + [top((2 * near, HEAD_DIM))] * 4 + [top(shares.shape)],
        out_specs=top((rows, HEAD_DIM)),
        compiler_params=pltpu.CompilerParams(vmem_limit_bytes=16 << 20),
    )(w_out, *heads, shares)


def unpack_kernel(moves, x_ref, quarter_ref, w_ref):
    deep = x_ref.shape[0]
    blocks = w_ref.shape[1] // HEAD_DIM
    rows = w_ref.shape[0] // deep
    base = blocks * rows
    near = BLOCK // 4 // deep
    share = BLOCK // 16
    for z in range(deep):
        for c in range(blocks):
            w_ref[z * rows : (z + 1) * rows, lanes(c)] = x_ref[z, c * rows : (c + 1) * rows, :]
    pairs = [x_ref[z, base : base + 4 * near, :].astype(F32) for z in range(deep)]
    moving = [
        jnp.concatenate([pair[n * near : (n + 1) * near] for pair in pairs], axis=0).astype(BF) for n in range(4)
    ]
    base += 4 * near
    still = [
        jnp.concatenate(
            [x_ref[z, base + n * share : base + (n + 1) * share, :] for z in range(0, deep, deep // 4)], axis=0
        )
        for n in range(4)
    ]
    flag = moves[0] > 0
    quarter_ref[:, lanes(0)] = moving[0]
    quarter_ref[:, lanes(2)] = moving[2]
    quarter_ref[:, lanes(4)] = still[1]
    quarter_ref[:, lanes(5)] = still[3]
    quarter_ref[:, lanes(1)] = jnp.where(flag, moving[1].astype(F32), still[0].astype(F32)).astype(BF)
    quarter_ref[:, lanes(3)] = jnp.where(flag, moving[3].astype(F32), still[2].astype(F32)).astype(BF)


def unpack(moves, x, w_rows, w_cols):
    return pl.pallas_call(
        unpack_kernel,
        out_shape=(
            jax.ShapeDtypeStruct((BLOCK // 4, 6 * HEAD_DIM), BF),
            jax.ShapeDtypeStruct((w_rows, w_cols), BF),
        ),
        in_specs=[SMEM, VMEM],
        out_specs=(VMEM, VMEM),
        compiler_params=pltpu.CompilerParams(vmem_limit_bytes=16 << 20),
        cost_estimate=pl.CostEstimate(flops=COVER, bytes_accessed=0, transcendentals=0),
    )(moves, x)


def order_kernel(order, w_ref, out_ref):
    for n in range(w_ref.shape[0] // HEAD_DIM):
        out_ref[n * HEAD_DIM : (n + 1) * HEAD_DIM, :] = w_ref[
            pl.ds(pl.multiple_of(order[n] * HEAD_DIM, HEAD_DIM), HEAD_DIM), :
        ]


def slot_order(order, w):
    return pl.pallas_call(
        order_kernel,
        out_shape=jax.ShapeDtypeStruct(w.shape, BF),
        in_specs=[SMEM, VMEM],
        out_specs=VMEM,
        compiler_params=pltpu.CompilerParams(vmem_limit_bytes=16 << 20),
    )(order, w)


def projection_kernel(attn_ref, w_ref, out_ref, total_ref):
    part = jnp.dot(attn_ref[...], w_ref[...], preferred_element_type=F32)
    step = pl.program_id(0)
    last = pl.num_programs(0) - 1

    @pl.when(step == 0)
    def _():
        total_ref[...] = part

    @pl.when((step > 0) & (step < last))
    def _():
        total_ref[...] += part

    @pl.when(step == last)
    def _():
        out_ref[...] = (total_ref[...] + part).astype(BF)


def projection(attn, w):
    rows, depth = attn.shape
    cols = w.shape[1]
    steps = 4
    return pl.pallas_call(
        projection_kernel,
        out_shape=jax.ShapeDtypeStruct((rows, cols), BF),
        grid=(steps,),
        in_specs=[
            pl.BlockSpec((rows, depth // steps), lambda i: (0, i)),
            pl.BlockSpec((depth // steps, cols), lambda i: (i, 0)),
        ],
        out_specs=pl.BlockSpec((rows, cols), lambda i: (0, 0)),
        scratch_shapes=[pltpu.VMEM((rows, cols), F32)],
        compiler_params=pltpu.CompilerParams(vmem_limit_bytes=56 << 20),
    )(attn, w)


def slots_of(labels):
    temporal = labels == 1
    a = jnp.where(temporal[:, 0], 0, jnp.where(temporal[:, 1], 1, 2))
    c = jnp.where(~temporal[:, 2], 2, jnp.where(~temporal[:, 1], 1, 0))
    return jnp.stack([a, 3 - a - c, c], axis=1).astype(jnp.int32)


def split_blocks(x):
    return jnp.concatenate([x[:BLOCK], x[BLOCK:]], axis=1)


def position_pack(x, parts):
    rows = x.shape[0] // parts // 2
    return x.reshape(parts, 2, rows, x.shape[1]).transpose(0, 2, 1, 3).reshape(parts, rows, 2 * x.shape[1])


def exchange(x):
    return lax.all_to_all(x, "ctx", 0, 0, tiled=True)


def both_ways(x, count):
    left = lax.ppermute(x, "ctx", [(i, i + 1) for i in range(count - 1)])
    right = lax.ppermute(x, "ctx", [(i + 1, i) for i in range(count - 1)])
    return left, right


def scattered(x, index, unit, live):
    count = lax.axis_size("ctx")
    rows = x.shape[0] // 4
    out = x[:rows]
    for k in (1, 2, 3):
        got = lax.ppermute(x[k * rows : (k + 1) * rows], "ctx", [(i, i + k * unit) for i in range(0, count, live)])
        out = jnp.where(index == k, got, out)
    return out


def body(queries, keys, values, block_mask, head_labels, w_out):
    parts = lax.axis_size("ctx")
    groups = lax.axis_size("head")
    place = lax.axis_index("ctx")
    group = lax.axis_index("head")
    deep = parts // 4
    y_lines = [[y * deep + z for y in range(4)] for z in range(deep)]
    along_z = [[y * deep + z for z in range(deep)] for y in range(4)]
    slots = slots_of(head_labels.reshape(groups, 3))
    mine = lax.dynamic_slice_in_dim(slots, group, 1, 0)[0]
    labels = lax.dynamic_slice_in_dim(head_labels, group * 3, 3)
    moves = lax.dynamic_slice_in_dim(labels, mine[1], 1)
    order = (slots + 3 * jnp.arange(groups, dtype=jnp.int32)[:, None]).reshape(-1)

    def head_of(x, slot):
        return lax.dynamic_slice_in_dim(x, mine[slot] * HEAD_DIM, HEAD_DIM, 1)

    q0, q1, q2 = (head_of(queries, s) for s in range(3))
    k0, k1, k2 = (head_of(keys, s) for s in range(3))
    v0, v1, v2 = (head_of(values, s) for s in range(3))

    index = place * 2 + jnp.arange(2, dtype=jnp.int32)
    total_blocks = block_mask.shape[0]
    rows = lax.dynamic_slice_in_dim(block_mask, place * 2, 2, 0)
    cand = index[:, None] + jnp.arange(-REACH, REACH + 1, dtype=jnp.int32)[None, :]
    every = jnp.arange(total_blocks, dtype=jnp.int32)
    hits = jnp.any((cand[:, :, None] == every[None, None, :]) & (rows[:, None, :] == 1), axis=2)
    first_bit = (index > REACH) & (rows[:, 0] == 1)
    bits = jnp.concatenate([hits, first_bit[:, None]], axis=1).astype(jnp.int32)

    shares = jnp.concatenate([k1, k2, v1, v2], axis=1)[:BLOCK]
    shares = scattered(shares, place // deep, deep, parts)
    shares = scattered(shares, place % deep // (deep // 4), deep // 4, deep)

    packs = [position_pack(jnp.concatenate(pair, axis=1), parts) for pair in ((q0, q1), (k0, k1), (v0, v1))]
    near = BLOCK // parts
    sent = payload(near, w_out, (k0, k1, v0, v1), shares)
    packed, sent = lax.optimization_barrier((jnp.concatenate(packs, axis=2), sent))
    moved = exchange(packed).reshape(BLOCK, -1)
    rows_z = lax.all_gather(sent, "ctx", axis=0, axis_index_groups=along_z)
    quarter, w_z = unpack(moves, rows_z, deep * w_out.shape[0], w_out.shape[1])
    q2, k2, v2, quarter = lax.optimization_barrier((q2, k2, v2, quarter))
    own2 = jnp.concatenate([split_blocks(k2), split_blocks(v2)], axis=1)
    query2 = split_blocks(q2)
    moved, quarter, own2 = lax.optimization_barrier((moved, quarter, own2))
    query, own = mix(moves, moved, (q1, k1, v1))
    left, right = both_ways(own, parts)

    def along_y(x):
        return [lax.ppermute(x, "ctx", [(i, i ^ (deep * k)) for i in range(parts)]) for k in (1, 2, 3)]

    first = [quarter] + along_y(quarter)
    left, right, first = lax.optimization_barrier((left, right, first))
    w_z, *first = lax.optimization_barrier((w_z, *first))
    w = lax.all_gather(w_z, "ctx", axis=0, axis_index_groups=y_lines, tiled=True)

    out = attention(2, bits, query, own, left, right, first)
    own2, _, _ = lax.optimization_barrier((own2, left, right))
    out, left2, right2 = lax.optimization_barrier((out, *both_ways(own2, parts)))
    out2 = attention(1, bits, query2, own2, left2, right2, first)
    attn2 = jnp.concatenate([out2[:, lanes(0)], out2[:, lanes(1)]], axis=0)

    back = exchange(out.reshape(parts, BLOCK // parts, -1))
    back = back.reshape(parts, BLOCK // parts, 2, 2 * HEAD_DIM).transpose(0, 2, 1, 3).reshape(2 * BLOCK, 2 * HEAD_DIM)
    still = jnp.concatenate([out[:, lanes(1)], out[:, lanes(3)]], axis=0)
    attn = jnp.concatenate([back[:, lanes(0)], jnp.where(moves[0] > 0, back[:, lanes(1)], still), attn2], axis=1)
    return projection(lax.all_gather(attn, "head", axis=1, tiled=True), slot_order(order, w))


def solution(mesh):
    return jax.shard_map(
        body,
        mesh=mesh,
        in_specs=(P("ctx", "head"), P("ctx", "head"), P("ctx", "head"), P(), P(), P("ctx", "head")),
        out_specs=P("ctx", "head"),
        check_vma=False,
    )
```

```python
import math

import jax
import jax.numpy as jnp
from jax import lax
from jax.experimental import pallas as pl
from jax.experimental.pallas import tpu as pltpu
from jax.sharding import PartitionSpec as P

HEAD_DIM = 128
BLOCK = 512
REACH = 2
BF = jnp.bfloat16
F32 = jnp.float32
RATE = math.log2(math.e) / math.sqrt(HEAD_DIM)
SPAN = 2 * REACH + 1
COVER = 1 << 36


def lanes(index):
    return slice(index * HEAD_DIM, (index + 1) * HEAD_DIM)


VMEM = pl.BlockSpec(memory_space=pltpu.VMEM)
SMEM = pl.BlockSpec(memory_space=pltpu.SMEM)


def attention_kernel(heads, bits, q_ref, own_ref, left_ref, right_ref, f0, f1, f2, f3, out_ref, s_ref, m_ref, l_ref, acc_ref):
    sides = (left_ref, left_ref, own_ref, own_ref, right_ref, right_ref)

    def tile(kind, b, n, slot):
        if n == SPAN:
            column = kind * 2 + slot if heads == 2 else 4 + kind
            return jnp.concatenate([f[:, lanes(column)] for f in (f0, f1, f2, f3)], axis=0)
        return sides[b + n][:, lanes((kind * 2 + (b + n) % 2) * heads + slot)]

    for slot in range(heads):
        for b in range(2):
            here = lanes(b * heads + slot)
            query = q_ref[:, here]
            m_ref[...] = jnp.full_like(m_ref, -jnp.inf)
            l_ref[...] = jnp.zeros_like(l_ref)
            acc_ref[...] = jnp.zeros_like(acc_ref)
            m = jnp.full_like(m_ref, -jnp.inf)
            for n in range(SPAN + 1):
                s = lax.dot_general(
                    query, tile(0, b, n, slot), (((1,), (1,)), ((), ())), preferred_element_type=F32
                )
                s = jnp.where(bits[b, n] > 0, s, -jnp.inf)
                s_ref[n] = s
                for c in range(BLOCK // HEAD_DIM):
                    m = jnp.maximum(m, s[:, lanes(c)])
            m_ref[...] = m

            m_ref[...] = jnp.broadcast_to(jnp.max(m_ref[...], axis=1, keepdims=True), m_ref.shape)
            peak = m_ref[...]
            total = jnp.zeros_like(l_ref)
            mixed = jnp.zeros_like(acc_ref)
            for n in range(SPAN + 1):
                parts = []
                for c in range(BLOCK // HEAD_DIM):
                    w = jnp.exp2((s_ref[n, :, lanes(c)] - peak) * RATE)
                    total = total + w
                    parts.append(w.astype(BF))
                mixed = mixed + jnp.dot(
                    jnp.concatenate(parts, axis=1), tile(1, b, n, slot), preferred_element_type=F32
                )
            l_ref[...] = total
            acc_ref[...] = mixed

            total = jnp.sum(l_ref[...], axis=1, keepdims=True)
            out_ref[:, here] = (acc_ref[...] / total).astype(BF)


def attention(heads, bits, query, own, left, right, first):
    pairs = heads * 2 * (SPAN + 1)
    return pl.pallas_call(
        lambda *refs: attention_kernel(heads, *refs),
        out_shape=jax.ShapeDtypeStruct(query.shape, BF),
        in_specs=[SMEM] + [VMEM] * 8,
        out_specs=VMEM,
        scratch_shapes=[
            pltpu.VMEM((SPAN + 1, BLOCK, BLOCK), F32),
            pltpu.VMEM((BLOCK, HEAD_DIM), F32),
            pltpu.VMEM((BLOCK, HEAD_DIM), F32),
            pltpu.VMEM((BLOCK, HEAD_DIM), F32),
        ],
        compiler_params=pltpu.CompilerParams(vmem_limit_bytes=32 << 20),
        cost_estimate=pl.CostEstimate(
            flops=pairs * 4 * BLOCK * BLOCK * HEAD_DIM,
            bytes_accessed=heads * 16 * BLOCK * HEAD_DIM * 2,
            transcendentals=pairs * BLOCK * BLOCK,
        ),
    )(bits, query, own, left, right, *first)


def mix_kernel(moves, moved_ref, q1_ref, k1_ref, v1_ref, query_ref, own_ref):
    kept = (q1_ref, k1_ref, v1_ref)

    def target(n):
        return (query_ref, lanes(n)) if n < 4 else (own_ref, lanes(n - 4))

    for n in range(12):
        out_ref, here = target(n)
        if n % 2 == 0:
            out_ref[:, here] = moved_ref[:, lanes(n)]

    @pl.when(moves[0] > 0)
    def _():
        for n in range(1, 12, 2):
            out_ref, here = target(n)
            out_ref[:, here] = moved_ref[:, lanes(n)]

    @pl.when(moves[0] <= 0)
    def _():
        for n in range(1, 12, 2):
            out_ref, here = target(n)
            b = n // 2 % 2
            out_ref[:, here] = kept[n // 4][b * BLOCK : (b + 1) * BLOCK, :]


def mix(moves, moved, kept):
    return pl.pallas_call(
        mix_kernel,
        out_shape=(
            jax.ShapeDtypeStruct((BLOCK, 4 * HEAD_DIM), BF),
            jax.ShapeDtypeStruct((BLOCK, 8 * HEAD_DIM), BF),
        ),
        in_specs=[SMEM] + [VMEM] * 4,
        out_specs=(VMEM, VMEM),
        compiler_params=pltpu.CompilerParams(vmem_limit_bytes=16 << 20),
    )(moves, moved, *kept)


def payload_kernel(w_ref, k0, k1, v0, v1, shares_ref, out_ref):
    rows = w_ref.shape[0]
    share = shares_ref.shape[0]
    at = 0
    for c in range(w_ref.shape[1] // HEAD_DIM):
        out_ref[at : at + rows, :] = w_ref[:, lanes(c)]
        at += rows
    for a, b in ((k0, k1), (v0, v1)):
        near = a.shape[0] // 2
        both = [x[...].astype(F32)[:near] for x in (a, b)]
        out_ref[at : at + 2 * near, :] = jnp.concatenate(both, axis=0).astype(BF)
        at += 2 * near
    for n in range(4):
        out_ref[at : at + share, :] = shares_ref[:, lanes(n)]
        at += share


def payload(near, w_out, heads, shares):
    rows = w_out.size // HEAD_DIM + 4 * near + shares.size // HEAD_DIM

    def top(shape):
        return pl.BlockSpec(shape, lambda i: (0, 0))

    return pl.pallas_call(
        payload_kernel,
        out_shape=jax.ShapeDtypeStruct((rows, HEAD_DIM), BF),
        grid=(1,),
        in_specs=[top(w_out.shape)] + [top((2 * near, HEAD_DIM))] * 4 + [top(shares.shape)],
        out_specs=top((rows, HEAD_DIM)),
        compiler_params=pltpu.CompilerParams(vmem_limit_bytes=16 << 20),
    )(w_out, *heads, shares)


def unpack_kernel(moves, x_ref, quarter_ref, w_ref):
    deep = x_ref.shape[0]
    blocks = w_ref.shape[1] // HEAD_DIM
    rows = w_ref.shape[0] // deep
    base = blocks * rows
    near = BLOCK // 4 // deep
    share = BLOCK // 16
    for z in range(deep):
        for c in range(blocks):
            w_ref[z * rows : (z + 1) * rows, lanes(c)] = x_ref[z, c * rows : (c + 1) * rows, :]
    pairs = [x_ref[z, base : base + 4 * near, :].astype(F32) for z in range(deep)]
    moving = [
        jnp.concatenate([pair[n * near : (n + 1) * near] for pair in pairs], axis=0).astype(BF) for n in range(4)
    ]
    base += 4 * near
    still = [
        jnp.concatenate(
            [x_ref[z, base + n * share : base + (n + 1) * share, :] for z in range(0, deep, deep // 4)], axis=0
        )
        for n in range(4)
    ]
    flag = moves[0] > 0
    quarter_ref[:, lanes(0)] = moving[0]
    quarter_ref[:, lanes(2)] = moving[2]
    quarter_ref[:, lanes(4)] = still[1]
    quarter_ref[:, lanes(5)] = still[3]
    quarter_ref[:, lanes(1)] = jnp.where(flag, moving[1].astype(F32), still[0].astype(F32)).astype(BF)
    quarter_ref[:, lanes(3)] = jnp.where(flag, moving[3].astype(F32), still[2].astype(F32)).astype(BF)


def unpack(moves, x, w_rows, w_cols):
    return pl.pallas_call(
        unpack_kernel,
        out_shape=(
            jax.ShapeDtypeStruct((BLOCK // 4, 6 * HEAD_DIM), BF),
            jax.ShapeDtypeStruct((w_rows, w_cols), BF),
        ),
        in_specs=[SMEM, VMEM],
        out_specs=(VMEM, VMEM),
        compiler_params=pltpu.CompilerParams(vmem_limit_bytes=16 << 20),
        cost_estimate=pl.CostEstimate(flops=COVER, bytes_accessed=0, transcendentals=0),
    )(moves, x)


def order_kernel(order, w_ref, out_ref):
    for n in range(w_ref.shape[0] // HEAD_DIM):
        out_ref[n * HEAD_DIM : (n + 1) * HEAD_DIM, :] = w_ref[
            pl.ds(pl.multiple_of(order[n] * HEAD_DIM, HEAD_DIM), HEAD_DIM), :
        ]


def slot_order(order, w):
    return pl.pallas_call(
        order_kernel,
        out_shape=jax.ShapeDtypeStruct(w.shape, BF),
        in_specs=[SMEM, VMEM],
        out_specs=VMEM,
        compiler_params=pltpu.CompilerParams(vmem_limit_bytes=16 << 20),
    )(order, w)


def slots_of(labels):
    temporal = labels == 1
    a = jnp.where(temporal[:, 0], 0, jnp.where(temporal[:, 1], 1, 2))
    c = jnp.where(~temporal[:, 2], 2, jnp.where(~temporal[:, 1], 1, 0))
    return jnp.stack([a, 3 - a - c, c], axis=1).astype(jnp.int32)


def split_blocks(x):
    return jnp.concatenate([x[:BLOCK], x[BLOCK:]], axis=1)


def position_pack(x, parts):
    rows = x.shape[0] // parts // 2
    return x.reshape(parts, 2, rows, x.shape[1]).transpose(0, 2, 1, 3).reshape(parts, rows, 2 * x.shape[1])


def exchange(x):
    return lax.all_to_all(x, "ctx", 0, 0, tiled=True)


def both_ways(x, count):
    left = lax.ppermute(x, "ctx", [(i, i + 1) for i in range(count - 1)])
    right = lax.ppermute(x, "ctx", [(i + 1, i) for i in range(count - 1)])
    return left, right


def scattered(x, index, unit, live):
    count = lax.axis_size("ctx")
    rows = x.shape[0] // 4
    out = x[:rows]
    for k in (1, 2, 3):
        got = lax.ppermute(x[k * rows : (k + 1) * rows], "ctx", [(i, i + k * unit) for i in range(0, count, live)])
        out = jnp.where(index == k, got, out)
    return out


def body(queries, keys, values, block_mask, head_labels, w_out):
    parts = lax.axis_size("ctx")
    groups = lax.axis_size("head")
    place = lax.axis_index("ctx")
    group = lax.axis_index("head")
    deep = parts // 4
    y_lines = [[y * deep + z for y in range(4)] for z in range(deep)]
    along_z = [[y * deep + z for z in range(deep)] for y in range(4)]
    slots = slots_of(head_labels.reshape(groups, 3))
    mine = lax.dynamic_slice_in_dim(slots, group, 1, 0)[0]
    labels = lax.dynamic_slice_in_dim(head_labels, group * 3, 3)
    moves = lax.dynamic_slice_in_dim(labels, mine[1], 1)
    order = (slots + 3 * jnp.arange(groups, dtype=jnp.int32)[:, None]).reshape(-1)

    def head_of(x, slot):
        return lax.dynamic_slice_in_dim(x, mine[slot] * HEAD_DIM, HEAD_DIM, 1)

    q0, q1, q2 = (head_of(queries, s) for s in range(3))
    k0, k1, k2 = (head_of(keys, s) for s in range(3))
    v0, v1, v2 = (head_of(values, s) for s in range(3))

    index = place * 2 + jnp.arange(2, dtype=jnp.int32)
    total_blocks = block_mask.shape[0]
    rows = lax.dynamic_slice_in_dim(block_mask, place * 2, 2, 0)
    cand = index[:, None] + jnp.arange(-REACH, REACH + 1, dtype=jnp.int32)[None, :]
    every = jnp.arange(total_blocks, dtype=jnp.int32)
    hits = jnp.any((cand[:, :, None] == every[None, None, :]) & (rows[:, None, :] == 1), axis=2)
    first_bit = (index > REACH) & (rows[:, 0] == 1)
    bits = jnp.concatenate([hits, first_bit[:, None]], axis=1).astype(jnp.int32)

    shares = jnp.concatenate([k1, k2, v1, v2], axis=1)[:BLOCK]
    shares = scattered(shares, place // deep, deep, parts)
    shares = scattered(shares, place % deep // (deep // 4), deep // 4, deep)

    packs = [position_pack(jnp.concatenate(pair, axis=1), parts) for pair in ((q0, q1), (k0, k1), (v0, v1))]
    near = BLOCK // parts
    sent = payload(near, w_out, (k0, k1, v0, v1), shares)
    packed, sent = lax.optimization_barrier((jnp.concatenate(packs, axis=2), sent))
    moved = exchange(packed).reshape(BLOCK, -1)
    rows_z = lax.all_gather(sent, "ctx", axis=0, axis_index_groups=along_z)
    quarter, w_z = unpack(moves, rows_z, deep * w_out.shape[0], w_out.shape[1])
    q2, k2, v2, quarter = lax.optimization_barrier((q2, k2, v2, quarter))
    own2 = jnp.concatenate([split_blocks(k2), split_blocks(v2)], axis=1)
    query2 = split_blocks(q2)
    moved, quarter, own2 = lax.optimization_barrier((moved, quarter, own2))
    query, own = mix(moves, moved, (q1, k1, v1))
    left, right = both_ways(own, parts)

    def along_y(x):
        return [lax.ppermute(x, "ctx", [(i, i ^ (deep * k)) for i in range(parts)]) for k in (1, 2, 3)]

    first = [quarter] + along_y(quarter)
    left, right, first = lax.optimization_barrier((left, right, first))
    w_z, *first = lax.optimization_barrier((w_z, *first))
    w = lax.all_gather(w_z, "ctx", axis=0, axis_index_groups=y_lines, tiled=True)

    out = attention(2, bits, query, own, left, right, first)
    own2, _, _ = lax.optimization_barrier((own2, left, right))
    out, left2, right2 = lax.optimization_barrier((out, *both_ways(own2, parts)))
    out2 = attention(1, bits, query2, own2, left2, right2, first)
    attn2 = jnp.concatenate([out2[:, lanes(0)], out2[:, lanes(1)]], axis=0)

    back = exchange(out.reshape(parts, BLOCK // parts, -1))
    back = back.reshape(parts, BLOCK // parts, 2, 2 * HEAD_DIM).transpose(0, 2, 1, 3).reshape(2 * BLOCK, 2 * HEAD_DIM)
    still = jnp.concatenate([out[:, lanes(1)], out[:, lanes(3)]], axis=0)
    attn = jnp.concatenate([back[:, lanes(0)], jnp.where(moves[0] > 0, back[:, lanes(1)], still), attn2], axis=1)
    everything = lax.all_gather(attn, "head", axis=1, tiled=True)
    return jnp.dot(everything, slot_order(order, w), preferred_element_type=F32).astype(BF)


def solution(mesh):
    return jax.shard_map(
        body,
        mesh=mesh,
        in_specs=(P("ctx", "head"), P("ctx", "head"), P("ctx", "head"), P(), P(), P("ctx", "head")),
        out_specs=P("ctx", "head"),
        check_vma=False,
    )
```
